32 devices in a mesh: img: 16 (over z, y, x), pix: 2 (over core).
Axes of the slice: x: 2, y: 2, z: 4, core: 2. Of those that a mesh axis runs over, the one named last changes fastest.
Arguments:
- images_in: bfloat16 [16, 32, 32, 384], P('img', 'pix'), may hold values from -6 to 6
- extents: int32 [16, 2], P('img'), may hold values from 8 to 32, as said below
- timesteps: int32 [16], P('img'), may hold values from 0 to 39
- gain_first: float32 [384], replicated, may hold values from 0.5 to 1.5
- shift_first: float32 [384], replicated, may hold values from -1.8 to 1.8
- kernel_first: bfloat16 [3, 3, 384, 384], replicated, may hold values from -0.109375 to 0.109375
- offset_first: float32 [384], replicated, may hold values from -1.8 to 1.8
- embed_weight: bfloat16 [768, 768], replicated, may hold values from -0.21875 to 0.21875
- embed_offset: float32 [768], replicated, may hold values from -1.8 to 1.8
- gain_second: float32 [384], replicated, may hold values from 0.5 to 1.5
- shift_second: float32 [384], replicated, may hold values from -1.8 to 1.8
- kernel_second: bfloat16 [3, 3, 384, 384], replicated, may hold values from -0.15625 to 0.15625
- offset_second: float32 [384], replicated, may hold values from -1.8 to 1.8
- gain_attend: float32 [384], replicated, may hold values from 0.5 to 1.5
- shift_attend: float32 [384], replicated, may hold values from -1.8 to 1.8
- project_in: bfloat16 [384, 1152], replicated, may hold values from -0.3125 to 0.3125
- offset_in: float32 [768], replicated, may hold values from -1.8 to 1.8
- project_out: bfloat16 [384, 384], replicated, may hold values from -3.5 to 3.5
- offset_out: float32 [384], replicated, may hold values from -1.8 to 1.8
- out_grad: bfloat16 [16, 32, 32, 384], P('img', 'pix'), may hold values from -6 to 6
Outputs:
- result: bfloat16 [16, 32, 32, 384], P('img', 'pix')
- in_grad: bfloat16 [16, 32, 32, 384], P('img', 'pix')
- grad_gain_first: float32 [384], replicated
- grad_shift_first: float32 [384], replicated
- grad_kernel_first: float32 [3, 3, 384, 384], replicated
- grad_offset_first: float32 [384], replicated
- grad_embed_weight: float32 [768, 768], replicated
- grad_embed_offset: float32 [768], replicated
- grad_gain_second: float32 [384], replicated
- grad_shift_second: float32 [384], replicated
- grad_kernel_second: float32 [3, 3, 384, 384], replicated
- grad_offset_second: float32 [384], replicated
- grad_gain_attend: float32 [384], replicated
- grad_shift_attend: float32 [384], replicated
- grad_project_in: float32 [384, 1152], replicated
- grad_offset_in: float32 [768], replicated
- grad_project_out: float32 [384, 384], replicated
- grad_offset_out: float32 [384], replicated
The draws below stay inside these ranges and needn't reach their ends.
Inputs may be any that keep to these rules, and one draw needn't show every extreme that they name: extents[i] = (valid rows, valid columns) of image i. Every image has more than 17 valid rows, and at least one image is valid at every pixel.
All inputs are finite; a program needn't handle non-finite values.
Results may differ from the reference program's by a relative error of at most 0.014.
Values may be sent and summed in bfloat16 or wider, within the bound.
A program may use at most 128 MiB of HBM per device.

```python
import math
import jax
import jax.numpy as jnp
from jax import lax

C = 384
HEADS = 6
HEAD_DIM = 64
TE = 768
GROUPS = 32
SIDE = 32
IMAGES = 16


def draw_extents(key, part):
    key = jax.random.fold_in(key, 11)
    key_rows, key_cols, key_pick = jax.random.split(key, 3)
    heights = jax.random.randint(key_rows, (IMAGES,), SIDE // 2 + 2, SIDE + 1)
    widths = jax.random.randint(key_cols, (IMAGES,), SIDE // 4, SIDE + 1)
    native = jax.random.randint(key_pick, (), 0, IMAGES)
    whole = jnp.arange(IMAGES) == native
    heights = jnp.where(whole, SIDE, heights)
    widths = jnp.where(whole, SIDE, widths)
    return jnp.stack([heights, widths], axis=1).astype(jnp.int32)


def place_ends(values, rng, smallest, high):
    longest = values.shape.index(max(values.shape))
    spots = []
    for shift in (0, 1):
        where = [jax.random.randint(jax.random.fold_in(rng, axis), (), 0, length) for axis, length in enumerate(values.shape)]
        where[longest] = (where[longest] + shift) % values.shape[longest]
        spots.append(tuple(where))
    return values.at[spots[0]].set(smallest).at[spots[1]].set(high)


def block_scale(rng, shape, cuts, least, largest):
    loudness, own = 1.0, jax.random.fold_in(rng, 6)
    for dim, shards_of in cuts:
        steps = jnp.exp(jax.random.uniform(jax.random.fold_in(own, dim), (shards_of,), jnp.float32, least / len(cuts), largest / len(cuts)))
        loudness = loudness * jnp.repeat(steps, shape[dim] // shards_of).reshape([-1 if axis == dim else 1 for axis in range(len(shape))])
    return loudness


def gaussian(rng, extent, deviation, limit, cuts=(), kind=jnp.bfloat16):
    level = block_scale(rng, extent, cuts, -0.22, 0.18) if cuts else 1.0
    drawn = jax.random.normal(rng, extent, jnp.float32) * deviation * level
    return jnp.minimum(jnp.maximum(drawn, -limit), limit).astype(kind)


def setup_inputs(seed: int = 0) -> dict:
    streams_of = jax.random.split(jax.random.key(seed), 21)
    return {
        "images_in": gaussian(streams_of[0], (IMAGES, SIDE, SIDE, C), 1.0, 6.0, ((0, 16), (1, 2))),
        "extents": draw_extents(jax.random.fold_in(streams_of[20], 71), 0),
        "timesteps": place_ends(jax.random.randint(streams_of[2], (IMAGES,), 0, 40), jax.random.fold_in(streams_of[2], 1), 0, 39).astype(jnp.int32),
        "gain_first": jnp.clip(jax.random.uniform(streams_of[3], (C,), jnp.float32, 0.5, 1.5), 0.5, 1.5),
        "shift_first": gaussian(streams_of[4], (C,), 0.3, 1.8, (), jnp.float32),
        "kernel_first": gaussian(streams_of[5], (3, 3, C, C), (9 * C) ** -0.5, 0.109375),
        "offset_first": gaussian(streams_of[6], (C,), 0.3, 1.8, (), jnp.float32),
        "embed_weight": gaussian(streams_of[7], (TE, 2 * C), TE ** -0.5, 0.21875),
        "embed_offset": gaussian(streams_of[8], (2 * C,), 0.3, 1.8, (), jnp.float32),
        "gain_second": jnp.clip(jax.random.uniform(streams_of[9], (C,), jnp.float32, 0.5, 1.5), 0.5, 1.5),
        "shift_second": gaussian(streams_of[10], (C,), 0.3, 1.8, (), jnp.float32),
        "kernel_second": gaussian(streams_of[11], (3, 3, C, C), (9 * C // 2) ** -0.5, 0.15625),
        "offset_second": gaussian(streams_of[12], (C,), 0.3, 1.8, (), jnp.float32),
        "gain_attend": jnp.clip(jax.random.uniform(streams_of[13], (C,), jnp.float32, 0.5, 1.5), 0.5, 1.5),
        "shift_attend": gaussian(streams_of[14], (C,), 0.3, 1.8, (), jnp.float32),
        "project_in": gaussian(streams_of[15], (C, 3 * C), C ** -0.5, 0.3125),
        "offset_in": gaussian(streams_of[16], (2 * C,), 0.3, 1.8, (), jnp.float32),
        "project_out": gaussian(streams_of[17], (C, C), (max(C // 128, 1)) ** -0.5, 3.5),
        "offset_out": gaussian(streams_of[18], (C,), 0.3, 1.8, (), jnp.float32),
        "out_grad": gaussian(streams_of[19], (IMAGES, SIDE, SIDE, C), 1.0, 6.0, ((0, 16), (1, 2))),
    }


@jax.custom_vjp
def low(v):
    return lax.optimization_barrier(v.astype(jnp.bfloat16)).astype(jnp.float32)

@jax.custom_vjp
def low_back(v):
    return v

def low_keep(v):
    return (low(v), None)

def low_pass(kept, grad):
    return (grad,)

def back_keep(v):
    return (v, None)

def back_low(kept, grad):
    return (low(grad),)
low.defvjp(low_keep, low_pass)
low_back.defvjp(back_keep, back_low)
PRECISE = lax.Precision.HIGHEST
EPSILON = 1e-05
MASKED = -1e+30

def time_features(timesteps, width):
    half_width = width // 2
    frequency = jnp.exp(-math.log(10000.0) * jnp.arange(half_width, dtype=jnp.float32) / half_width)
    angles = timesteps.astype(jnp.float32)[:, None] * frequency[None, :]
    return jnp.concatenate([jnp.cos(angles), jnp.sin(angles)], axis=1)

def pixel_masks(extents):
    position = jnp.arange(SIDE, dtype=jnp.int32)
    row_ok = position[None, :] < extents[:, 0:1]
    col_ok = position[None, :] < extents[:, 1:2]
    return (row_ok[:, :, None] & col_ok[:, None, :]).astype(jnp.float32)

def group_norm(field, pixel_mask, gain, bias_vec):
    batch = field.shape[0]
    grouped = field.reshape(batch, SIDE, SIDE, GROUPS, C // GROUPS)
    weight = pixel_mask[:, :, :, None, None]
    entries = lax.optimization_barrier(jnp.sum(pixel_mask, axis=(1, 2))) * (C // GROUPS)
    group_mean = lax.optimization_barrier(jnp.sum(grouped * weight, axis=(1, 2, 4))) / entries[:, None]
    squares = lax.optimization_barrier(jnp.sum(grouped * grouped * weight, axis=(1, 2, 4))) / entries[:, None]
    inv_std = lax.rsqrt(squares - group_mean * group_mean + EPSILON)
    normed = (grouped - group_mean[:, None, None, :, None]) * inv_std[:, None, None, :, None]
    return normed.reshape(field.shape) * gain + bias_vec

def convolve(acts, kernel):
    return lax.conv_general_dilated(acts, kernel, (1, 1), ((1, 1), (1, 1)), dimension_numbers=('NHWC', 'HWIO', 'NHWC'), precision=PRECISE)

def forward(pixels_in, time_vec, pixel_mask, param_set):
    gain_first, shift_first, kernel_first, offset_first, embed_weight, embed_offset, gain_second, shift_second, kernel_second, offset_second, gain_attend, shift_attend, project_in, offset_in, project_out, offset_out = param_set
    batch = pixels_in.shape[0]
    act_one = low(jax.nn.silu(group_norm(pixels_in, pixel_mask, gain_first, shift_first)))
    conv_one = low_back(convolve(act_one, kernel_first) + offset_first)
    film = jnp.dot(jax.nn.silu(time_vec), embed_weight, precision=PRECISE) + embed_offset
    film_scale = film[:, None, None, :C]
    film_shift = film[:, None, None, C:]
    pre_two = group_norm(conv_one, pixel_mask, gain_second, shift_second) * (1.0 + film_scale) + film_shift
    act_two = low(jax.nn.silu(pre_two))
    conv_two = low_back(convolve(act_two, kernel_second) + offset_second)
    hidden = pixels_in + conv_two
    att_in = low(group_norm(hidden, pixel_mask, gain_attend, shift_attend))
    pairs = offset_in.reshape(HEADS, 2, HEAD_DIM)
    key_zeros = jnp.zeros((HEADS, 1, HEAD_DIM), jnp.float32)
    bias_full = jnp.concatenate([pairs[:, 0:1], key_zeros, pairs[:, 1:2]], axis=1).reshape(3 * C)
    qkv = jnp.dot(att_in.reshape(batch * SIDE * SIDE, C), project_in, precision=PRECISE) + bias_full
    qkv = low(low_back(qkv)).reshape(batch, SIDE * SIDE, HEADS, 3, HEAD_DIM)
    queries = qkv[:, :, :, 0]
    key_vecs = qkv[:, :, :, 1]
    values = qkv[:, :, :, 2]
    scores = low_back(jnp.einsum('bqhd,bkhd->bhqk', queries, key_vecs, precision=PRECISE) / math.sqrt(HEAD_DIM))
    key_valid = pixel_mask.reshape(batch, 1, 1, SIDE * SIDE)
    scores = jnp.where(key_valid > 0, scores, MASKED)
    maxima = lax.optimization_barrier(jnp.max(scores, axis=-1, keepdims=True))
    shifted_exp = jnp.exp(scores - maxima)
    probabilities = low(shifted_exp / lax.optimization_barrier(jnp.sum(shifted_exp, axis=-1, keepdims=True)))
    attended = jnp.einsum('bhqk,bkhd->bqhd', probabilities, values, precision=PRECISE)
    attended = low(low_back(attended)).reshape(batch * SIDE * SIDE, C)
    projected = jnp.dot(attended, project_out, precision=PRECISE) + offset_out
    return hidden + projected.reshape(pixels_in.shape)

def reference(images_in, extents, timesteps, gain_first, shift_first, kernel_first, offset_first, embed_weight, embed_offset, gain_second, shift_second, kernel_second, offset_second, gain_attend, shift_attend, project_in, offset_in, project_out, offset_out, out_grad):
    param_set = tuple((w.astype(jnp.float32) for w in (gain_first, shift_first, kernel_first, offset_first, embed_weight, embed_offset, gain_second, shift_second, kernel_second, offset_second, gain_attend, shift_attend, project_in, offset_in, project_out, offset_out)))
    steps_count = IMAGES // 4
    pixels_all = images_in.astype(jnp.float32).reshape(steps_count, 4, SIDE, SIDE, C)
    grads_all = out_grad.astype(jnp.float32).reshape(steps_count, 4, SIDE, SIDE, C)
    times_all = time_features(timesteps, TE).reshape(steps_count, 4, TE)
    masks_all = pixel_masks(extents).reshape(steps_count, 4, SIDE, SIDE)

    def one_step(totals, block):
        pixels_in, cotangent, time_vec, pixel_mask = block

        def wrapped(inputs_now, params_now):
            return forward(inputs_now, time_vec, pixel_mask, params_now)
        outputs, pullback = jax.vjp(wrapped, pixels_in, param_set)
        input_grad, param_grads = pullback(cotangent)
        totals = jax.tree.map(lambda left, right: left + right, totals, param_grads)
        return (totals, (outputs.astype(jnp.bfloat16), input_grad.astype(jnp.bfloat16)))
    start = tuple((jnp.zeros_like(w) for w in param_set))
    totals, (outputs, input_grads) = lax.scan(one_step, start, (pixels_all, grads_all, times_all, masks_all))
    result = outputs.reshape(IMAGES, SIDE, SIDE, C)
    in_grad = input_grads.reshape(IMAGES, SIDE, SIDE, C)
    return (result, in_grad, totals[0], totals[1], totals[2], totals[3], totals[4], totals[5], totals[6], totals[7], totals[8], totals[9], totals[10], totals[11], totals[12], totals[13], totals[14], totals[15])
```

```python
import functools
import math

import jax
import jax.numpy as jnp
from jax import lax
from jax.experimental import pallas as pl
from jax.experimental.pallas import tpu as pltpu
from jax.sharding import PartitionSpec as P

HEAD_DIM = 64
GROUPS = 32
EPSILON = 1e-05
MASKED = -1e30
BF = jnp.bfloat16
F32 = jnp.float32
MESH = pl.DeviceIdType.MESH
WIN = 256
LANES = 128
RC = 128
MC = 256
QC = 256


def dot(a, b):
    return jnp.dot(a, b, preferred_element_type=F32)


def dot_nt(a, b):
    return lax.dot_general(a, b, (((1,), (1,)), ((), ())), preferred_element_type=F32)


def dot_hi(a, b):
    return jnp.dot(a, b, preferred_element_type=F32, precision=lax.Precision.HIGHEST)


def fold(v):
    return jnp.sum(v.reshape(v.shape[0] // 8, 8, v.shape[1]), axis=0)


def sigmoid(v):
    return 1.0 / (1.0 + jnp.exp(-v))


def cdiv(a, b):
    return -(-a // b)


class Flow:
    def __init__(self, pay, rbuf, out, base, rows, order, sems, core, img):
        self.pay, self.rbuf, self.out, self.lo, self.size = pay, rbuf, out, base, rows
        self.rbase = base
        self.order, self.sems, self.core, self.img = order, sems, core, img
        self.steps = len(order)
        self.k = -1
        self.cp = None
        self.fwd = []

    def peer(self, bit):
        mine = (self.img // bit) % 2
        return self.img + bit * (1 - 2 * mine), mine

    def sem(self, k):
        send, recv, first = self.sems
        return send.at[first + k], recv.at[first + k]

    def forward(self, lo, size, k):
        s, r = self.sem(k)
        ref = self.out.at[self.core, pl.ds(pl.multiple_of(lo, 16), size)]
        cp = pltpu.make_async_remote_copy(
            src_ref=ref, dst_ref=ref, send_sem=s, recv_sem=r, device_id=(self.img, 1 - self.core), device_id_type=MESH
        )
        cp.start()
        self.fwd.append(cp)

    def start(self):
        k = self.k
        n = self.steps
        s, r = self.sem(k)
        if k < n:
            peer, mine = self.peer(self.order[k])
            half = self.size // 2
            self.keep = pl.multiple_of(self.lo + mine * half, 16)
            send = pl.multiple_of(self.lo + (1 - mine) * half, 16)
            src = self.pay.at[pl.ds(send, half)]
            dst = self.rbuf.at[pl.ds(self.rbase, half)]
        else:
            peer, mine = self.peer(self.order[2 * n - 1 - k])
            self.mine = mine
            src = self.out.at[self.core, pl.ds(self.lo, self.size)]
            dst = src
        self.cp = pltpu.make_async_remote_copy(
            src_ref=src, dst_ref=dst, send_sem=s, recv_sem=r, device_id=(peer, self.core), device_id_type=MESH
        )
        self.cp.start()

    def finish(self):
        k, n = self.k, self.steps
        self.cp.wait()
        if k < n:
            half = self.size // 2
            keep, rbase = self.keep, self.rbase
            step = 16
            for cand in (512, 256, 128, 64, 32):
                if half % cand == 0:
                    step = cand
                    break

            def add(j, _):
                at = pl.ds(pl.multiple_of(keep + j * step, 16), step)
                rat = pl.ds(pl.multiple_of(rbase + j * step, 16), step)
                v = (self.pay[at, :].astype(F32) + self.rbuf[rat, :].astype(F32)).astype(BF)
                if k == n - 1:
                    self.out[self.core, at, :] = v
                else:
                    self.pay[at, :] = v
                return 0

            lax.fori_loop(0, half // step, add, 0)
            self.lo, self.size = keep, half
            self.rbase += half
        else:
            sib = self.lo + (1 - 2 * self.mine) * self.size
            if k == 2 * n - 1:
                self.forward(self.lo, self.size, 2 * n)
                self.forward(sib, self.size, 2 * n + 1)
            self.lo = pl.multiple_of(self.lo - self.mine * self.size, 16)
            self.size *= 2

    def advance(self):
        if self.k >= 2 * self.steps:
            return
        if self.k >= 0:
            self.finish()
        self.k += 1
        if self.k < 2 * self.steps:
            self.start()

    def wait_forward(self):
        for cp in self.fwd:
            cp.wait()


def block_kernel(dims, *refs):
    side, chans, n_img, real_k, real_p, bits = dims
    (
        x_in, g_in, ext, p_g1, p_s1, p_o1, p_g2, p_s2, p_o2, p_g3, p_s3, p_oo, t_act, e_off, off_in, k1_h, k2_h, wi_h, wo_h, ew_h,
        res_out, ing_out, pk1_o, pk2_o, pp_o, vec_o,
        k1, k2, wo, ew, wq, xw, gf, mask, film, act1, act2, act3, dd2, dd1,
        cv, hid, tmp, resid, qa, ka, va, kat, vat, dot_t, att_t, dk, dv, dqt, dqkv,
        tsum, trecv, datt_s, datt_r, dm, act_t, ing_r,
        pay1, pay2, payp, rb1, rb2, rbp, out1, out2, outp, vx, vr, vall,
        lsem, xs, xr, fs, fr,
    ) = refs
    img = lax.axis_index("img")
    c = lax.axis_index("pix")
    oc = 1 - c
    px = side * side
    half = px // 2
    own_chans = chans // 2
    heads = own_chans // HEAD_DIM
    first = c == 0
    nbits = len(bits)

    def aligned(v, m):
        return pl.multiple_of(v, m)

    def rows_at(j, size):
        return pl.ds(aligned(j * size, size), size)

    def pad_at(j, size, shift=side):
        return pl.ds(aligned(j * size + shift, 32), size)

    win = pl.ds(aligned(LANES * c, LANES), WIN)
    owin = pl.ds(aligned(LANES * oc, LANES), WIN)

    barrier = pltpu.get_barrier_semaphore()
    peers = [(img, oc)]
    for bit in bits:
        peers.append((img + bit * (1 - 2 * ((img // bit) % 2)), c))
    for peer in peers:
        pl.semaphore_signal(barrier, inc=1, device_id=peer, device_id_type=MESH)

    loads = []
    for k, (src, dst) in enumerate(((wi_h, dqkv.at[pl.ds(0, chans)]), (ew_h, ew), (wo_h, wo.at[pl.ds(0, chans)]), (k1_h, k1), (k2_h, k2))):
        cp = pltpu.make_async_copy(src, dst, lsem.at[k])
        cp.start()
        loads.append(cp)
    pl.semaphore_wait(barrier, len(peers))

    def swap(src, dst, k):
        cp = pltpu.make_async_remote_copy(
            src_ref=src, dst_ref=dst, send_sem=xs.at[k], recv_sem=xr.at[k], device_id=(img, oc), device_id_type=MESH
        )
        cp.start()
        return cp

    my_rows = pl.ds(aligned(half * c, half), half)
    other_rows = pl.ds(aligned(half * oc, half), half)
    swap_x = swap(x_in.at[:, owin], xw.at[my_rows], 0)
    swap_g = swap(g_in, gf.at[my_rows], 1)
    xw[my_rows, :] = x_in[:, win]
    gf[my_rows, :] = g_in[...]

    lane = lax.broadcasted_iota(jnp.int32, (1, WIN), 1)
    own_f = (jnp.where(first, lane, WIN - 1 - lane) < own_chans).astype(F32)
    rows_e = ext[0, 0]
    cols_e = ext[0, 1]
    per = chans // GROUPS
    inv_entries = 1.0 / jnp.full((1, WIN), rows_e * cols_e * per, jnp.int32).astype(F32)
    gi = lax.broadcasted_iota(jnp.int32, (WIN, WIN), 0) + LANES * c
    gj = lax.broadcasted_iota(jnp.int32, (WIN, WIN), 1) + LANES * c
    same = (gi // per == gj // per).astype(F32)

    def pvec(ref):
        return ref[win].reshape(1, WIN)

    gain1, shift1, offset1 = pvec(p_g1), pvec(p_s1), pvec(p_o1)
    gain2, shift2, offset2 = pvec(p_g2), pvec(p_s2), pvec(p_o2)
    gain3, shift3 = pvec(p_g3), pvec(p_s3)

    def group_totals(a, b):
        both = dot_hi(jnp.concatenate([a, b], axis=0), same)
        return jnp.sum(both[:8], axis=0, keepdims=True), jnp.sum(both[8:], axis=0, keepdims=True)

    def total(a):
        return jnp.sum(a, axis=0, keepdims=True)

    zero8 = jnp.zeros((8, WIN), F32)

    def fill_mask(j, _):
        p = lax.broadcasted_iota(jnp.int32, (RC, LANES), 0) + j * RC
        ok = (p // side < rows_e) & (p % side < cols_e)
        mask[rows_at(j, RC), :] = ok.astype(F32)
        return 0

    lax.fori_loop(0, px // RC, fill_mask, 0)

    def mask2(j, size=RC):
        m = mask[rows_at(j, size), :]
        return jnp.concatenate([m, m], axis=1)

    edge = jnp.zeros((side, WIN), BF)
    for buf in (act1, act2, dd2, dd1):
        for s in range(2):
            buf[s, pl.ds(0, side), :] = edge
            buf[s, pl.ds(side + px, side), :] = edge
    for b in range(3):
        dm[b, pl.ds(0, side), :] = edge
        dm[b, pl.ds(side + px, side), :] = edge
    for pay, real in ((pay1, real_k), (pay2, real_k), (payp, real_p)):
        rest = pay.shape[0] - real
        if rest:
            pay[pl.ds(real, rest), :] = jnp.zeros((rest, LANES), BF)
    wo[pl.ds(chans, WIN - own_chans), :] = jnp.zeros((WIN - own_chans, chans), BF)
    for h in range(heads):
        dot_t[h, pl.ds(HEAD_DIM, HEAD_DIM), :] = jnp.zeros((HEAD_DIM, px), BF)
    att_t[pl.ds(own_chans, WIN - own_chans), :] = jnp.zeros((WIN - own_chans, px), BF)
    vx[...] = jnp.zeros(vx.shape, F32)

    lane1 = lax.broadcasted_iota(jnp.int32, (1, LANES), 1)
    low1 = lane1 < HEAD_DIM
    loads[0].wait()
    for k in range(3 * heads):
        place = 3 * heads * c + k
        blk = dqkv[pl.ds(0, chans), pl.ds(aligned((place // 2) * LANES, LANES), LANES)].astype(F32)
        blk = jnp.where(place % 2 == 0, blk, pltpu.roll(blk, HEAD_DIM, 1))
        wq[:, pl.ds(k * LANES, LANES)] = jnp.where(low1, blk, 0.0).astype(BF)

    loads[1].wait()
    t = t_act[...]
    t_a = t.astype(BF).astype(F32)
    t_b = (t - t_a).astype(BF).astype(F32)
    row16 = lax.broadcasted_iota(jnp.int32, (16, t.shape[1]), 0)
    t_rows = jnp.where(row16 == 0, t_a, jnp.where(row16 == 1, t_b, jnp.where(row16 == 2, t - t_a - t_b, 0.0)))
    film[...] = total(dot(t_rows.astype(BF), ew[...])) + e_off[...].reshape(1, -1)
    scale2 = 1.0 + film[:, win]
    move2 = film[:, pl.ds(aligned(chans + LANES * c, LANES), WIN)]

    swap_x.wait()

    def stats_step(v, m, carry):
        vm = v * m
        return carry[0] + fold(vm), carry[1] + fold(vm * v)

    def moments(carry):
        s, q = group_totals(*carry)
        mean = s * inv_entries
        return mean, lax.rsqrt(q * inv_entries - mean * mean + EPSILON)

    def body(j, carry):
        return stats_step(xw[rows_at(j, RC), :].astype(F32), mask2(j), carry)

    mean1, rstd1 = moments(lax.fori_loop(0, px // RC, body, (zero8, zero8)))
    mul1 = rstd1 * gain1
    add1 = shift1 - mean1 * mul1

    def body(j, _):
        pre = xw[rows_at(j, RC), :].astype(F32) * mul1 + add1
        act1[c, pad_at(j, RC), :] = (pre * sigmoid(pre) * own_f).astype(BF)
        return 0

    lax.fori_loop(0, px // RC, body, 0)
    inner = pl.ds(side, px)
    swap_a1 = swap(act1.at[c, inner], act1.at[c, inner], 2)

    loads[2].wait()
    swap_g.wait()
    wo_rows = pl.ds(aligned(own_chans * c, HEAD_DIM), own_chans)

    def body(j, _):
        o = dot_nt(wo[wo_rows, :], gf[rows_at(j, QC), :])
        for h in range(heads):
            dot_t[h, pl.ds(0, HEAD_DIM), rows_at(j, QC)] = o[HEAD_DIM * h : HEAD_DIM * (h + 1)].astype(BF)
        return 0

    lax.fori_loop(0, px // QC, body, 0)

    col = lax.broadcasted_iota(jnp.int32, (MC, WIN), 0) % side
    not_first = (col != 0).astype(F32)
    not_last = (col != side - 1).astype(F32)

    def conv(acts, s, kern, back, j):
        accs = []
        for b in range(3):
            acc = None
            for a in range(3):
                lhs = acts[s, pl.ds(aligned(j * MC + side * a, 32), MC), :]
                if back:
                    tap = (2 - a) * 3 + 2 - b
                    rhs = kern[pl.ds(aligned(tap * chans + LANES * c, LANES), WIN), pl.ds(aligned(LANES * s, LANES), WIN)]
                    o = dot_nt(lhs, rhs)
                else:
                    tap = a * 3 + b
                    rhs = kern[pl.ds(aligned(tap * chans + LANES * s, LANES), WIN), win]
                    o = dot(lhs, rhs)
                acc = o if acc is None else acc + o
            accs.append(acc)
        return accs[1] + pltpu.roll(accs[0], 1, 0) * not_first + pltpu.roll(accs[2], MC - 1, 0) * not_last

    loads[3].wait()

    def body(j, _):
        cv[rows_at(j, MC), :] = conv(act1, c, k1, False, j)
        return 0

    lax.fori_loop(0, px // MC, body, 0)
    swap_a1.wait()

    def body(j, carry):
        v = cv[rows_at(j, MC), :] + conv(act1, oc, k1, False, j) + offset1
        cv[rows_at(j, MC), :] = v
        return stats_step(v, mask2(j, MC), carry)

    mean2, rstd2 = moments(lax.fori_loop(0, px // MC, body, (zero8, zero8)))
    mul2 = rstd2 * gain2 * scale2
    add2 = (shift2 - mean2 * rstd2 * gain2) * scale2 + move2

    def body(j, _):
        pre = cv[rows_at(j, RC), :] * mul2 + add2
        act2[c, pad_at(j, RC), :] = (pre * sigmoid(pre) * own_f).astype(BF)
        return 0

    lax.fori_loop(0, px // RC, body, 0)
    swap_a2 = swap(act2.at[c, inner], act2.at[c, inner], 3)

    loads[4].wait()

    def body(j, _):
        at = rows_at(j, MC)
        hid[at, :] = conv(act2, c, k2, False, j) + offset2 + xw[at, :].astype(F32)
        return 0

    lax.fori_loop(0, px // MC, body, 0)
    swap_a2.wait()

    def body(j, carry):
        v = hid[rows_at(j, MC), :] + conv(act2, oc, k2, False, j)
        hid[rows_at(j, MC), :] = v
        return stats_step(v, mask2(j, MC), carry)

    mean3, rstd3 = moments(lax.fori_loop(0, px // MC, body, (zero8, zero8)))
    mul3 = rstd3 * gain3
    add3 = shift3 - mean3 * mul3

    def body(j, _):
        act3[c, rows_at(j, RC), :] = ((hid[rows_at(j, RC), :] * mul3 + add3) * own_f).astype(BF)
        return 0

    lax.fori_loop(0, px // RC, body, 0)
    swap_a3 = swap(act3.at[c], act3.at[c], 4)

    biases = []
    for h in range(heads):
        blk = off_in[pl.ds(aligned(LANES * (heads * c + h), LANES), LANES)].reshape(1, LANES)
        turned = pltpu.roll(jnp.broadcast_to(blk, (8, LANES)), HEAD_DIM, 1)[:1]
        bias_q = jnp.where(low1, blk, jnp.where(lane1 == HEAD_DIM, 8.0, 0.0))
        bias_v = jnp.where(low1, turned, jnp.where(lane1 < HEAD_DIM + 2, 1.0, 0.0))
        biases.append((bias_q, bias_v))
    swap_a3.wait()

    def body(j, _):
        at = rows_at(j, MC)
        a0 = act3[0, at, :]
        a1 = act3[1, at, :]
        hidden_key = (mask[at, :] == 0.0) & (lane1 == HEAD_DIM)
        for h in range(heads):
            cols = pl.ds(3 * LANES * h, 3 * LANES)
            o = dot(a0, wq[pl.ds(0, WIN), cols]) + dot(a1, wq[pl.ds(LANES, WIN), cols])
            q = (o[:, :LANES] + biases[h][0]).astype(BF).astype(F32) * 0.125
            k = jnp.where(hidden_key, MASKED, o[:, LANES : 2 * LANES])
            v = o[:, 2 * LANES :] + biases[h][1]
            qa[h, at, :] = q.astype(BF)
            ka[h, at, :] = k.astype(BF)
            va[h, at, :] = v.astype(BF)
            kat[h, :, at] = k.T.astype(BF)
            vat[h, :, at] = v.T.astype(BF)
        return 0

    lax.fori_loop(0, px // MC, body, 0)

    dk[...] = jnp.zeros(dk.shape, F32)
    dv[...] = jnp.zeros(dv.shape, F32)
    row128 = lax.broadcasted_iota(jnp.int32, (LANES, QC), 0)

    def body(it, _):
        h = it // (px // QC)
        j = it % (px // QC)
        at = rows_at(j, QC)
        qc = qa[h, at, :]
        scores = dot_nt(ka[h], qc)
        top = jnp.max(scores, axis=0, keepdims=True)
        e = jnp.exp(scores - top).astype(BF)
        o = dot(vat[h], e)
        inv = 1.0 / o[HEAD_DIM : HEAD_DIM + 1, :]
        o = o * inv
        att_t[pl.ds(aligned(HEAD_DIM * h, HEAD_DIM), HEAD_DIM), at] = o[:HEAD_DIM].astype(BF)
        g = dot_t[h, :, at].astype(F32)
        less = -inv * jnp.sum(g * o, axis=0, keepdims=True)
        high = less.astype(BF).astype(F32)
        g = jnp.where(row128 == HEAD_DIM, high, jnp.where(row128 == HEAD_DIM + 1, less - high, g * inv)).astype(BF)
        ds = (e.astype(F32) * dot(va[h], g)).astype(BF)
        dv[h] += dot_nt(e, g)
        dk[h] += dot(ds, qc)
        dqt[h, :, at] = dot(kat[h], ds)
        return 0

    lax.fori_loop(0, heads * (px // QC), body, 0)

    for h in range(heads):

        def body(j, carry, h=h):
            at = rows_at(j, MC)
            parts = (dqt[h, :, at].T * 0.125, dk[h, at, :], dv[h, at, :])
            parts = [jnp.where(low1, p, 0.0).astype(BF) for p in parts]
            for k, p in enumerate(parts):
                dqkv[at, pl.ds((3 * h + k) * LANES, LANES)] = p
            return carry[0] + fold(parts[0].astype(F32)), carry[1] + fold(parts[2].astype(F32))

        z = jnp.zeros((8, LANES), F32)
        sum_q, sum_v = lax.fori_loop(0, px // MC, body, (z, z))
        sums = total(sum_q + pltpu.roll(sum_v, HEAD_DIM, 1))
        vx[pl.ds(13, 1), pl.ds(LANES * h, LANES)] = jnp.where(first, sums, 0.0)
        vx[pl.ds(14, 1), pl.ds(LANES * h, LANES)] = jnp.where(first, 0.0, sums)

    def body(j, _):
        at = rows_at(j, MC)
        datt_s[at, :] = dot_nt(dqkv[at, :], wq[owin, :]).astype(BF)
        return 0

    lax.fori_loop(0, px // MC, body, 0)
    swap_da = swap(datt_s, datt_r, 5)

    def body(j, _):
        at = rows_at(j, MC)
        tmp[at, :] = dot_nt(dqkv[at, :], wq[win, :])
        return 0

    lax.fori_loop(0, px // MC, body, 0)

    def turn(acts, shift):
        def body(j, _):
            a0 = acts[0, pad_at(j, MC, shift), :].astype(F32)
            a1 = acts[1, pad_at(j, MC, shift), :].astype(F32)
            at = rows_at(j, MC)
            act_t[pl.ds(0, LANES), at] = a0[:, :LANES].T.astype(BF)
            act_t[pl.ds(LANES, LANES), at] = (a0[:, LANES:] + a1[:, :LANES]).T.astype(BF)
            act_t[pl.ds(2 * LANES, LANES), at] = a1[:, LANES:].T.astype(BF)
            return 0

        lax.fori_loop(0, px // MC, body, 0)

    turn(act3, 0)
    for k in range(3 * heads // 2):
        o = dot(act_t[...], dqkv[:, pl.ds(2 * LANES * k, 2 * LANES)])
        pair = o[:, :LANES] + pltpu.roll(o[:, LANES:], HEAD_DIM, 1)
        payp[pl.ds(k * chans, chans), :] = pair.astype(BF)
    base = (3 * heads // 2) * chans
    if (3 * heads) % 2:
        o = dot(act_t[...], dqkv[:, pl.ds((3 * heads - 1) * LANES, LANES)])
        pair = o[: chans // 2] + pltpu.roll(o[chans // 2 :], HEAD_DIM, 1)
        payp[pl.ds(base, chans // 2), :] = pair.astype(BF)
        base += chans // 2
    o = dot(att_t[pl.ds(0, own_chans), :], gf[...])
    for b in range(chans // LANES):
        payp[pl.ds(base + b * own_chans, own_chans), :] = o[:, b * LANES : (b + 1) * LANES].astype(BF)

    used = [0]

    def flows(pay, rbuf, gathered):
        rows = pay.shape[0]
        units = rows // (16 * n_img)
        cut = (units // 2) * 16 * n_img
        swapped = [bits[1], bits[0]] + list(bits[2:])
        out = []
        for base, size, order in ((0, cut, list(bits)), (cut, rows - cut, swapped)):
            if size:
                out.append(Flow(pay, rbuf, gathered, base, size, order, (fs, fr, used[0]), c, img))
            used[0] += 2 * nbits + 2
        return out

    running = flows(payp, rbp, outp)

    def step():
        for flow in running:
            flow.advance()

    step()

    def body(j, _):
        at = rows_at(j, MC)
        tsum[at, :] = dot(att_t[:, at].astype(F32).T.astype(BF), wo[pl.ds(aligned(own_chans * c, HEAD_DIM), WIN), :])
        tsum[at, win] += hid[at, :] * own_f
        return 0

    lax.fori_loop(0, px // MC, body, 0)
    swap_t = swap(tsum.at[other_rows], trecv, 6)
    step()

    swap_da.wait()

    def back_sums(carry, u, normed):
        return carry[0] + fold(u), carry[1] + fold(u * normed)

    def body(j, carry):
        at = rows_at(j, RC)
        u = tmp[at, :] + datt_r[at, :].astype(F32)
        tmp[at, :] = u
        return back_sums(carry, u, (hid[at, :] - mean3) * rstd3)

    s0, s1 = lax.fori_loop(0, px // RC, body, (zero8, zero8))
    vx[pl.ds(6, 1), win] = total(s1) * own_f
    vx[pl.ds(7, 1), win] = total(s0) * own_f

    def spread_of(s0, s1, gain):
        a, b = group_totals(s0 * gain, s1 * gain)
        return a * inv_entries, b * inv_entries

    sp_a, sp_b = spread_of(s0, s1, gain3)

    def body(j, carry):
        at = rows_at(j, RC)
        normed = (hid[at, :] - mean3) * rstd3
        d = gf[at, win].astype(F32) + rstd3 * (tmp[at, :] * gain3 - mask2(j) * (sp_a + normed * sp_b))
        resid[at, :] = d
        low = (d * own_f).astype(BF)
        dd2[c, pad_at(j, RC), :] = low
        return carry + fold(low.astype(F32))

    vx[pl.ds(5, 1), win] = total(lax.fori_loop(0, px // RC, body, zero8))
    swap_d2 = swap(dd2.at[c, inner], dd2.at[c, inner], 7)
    step()

    def body(j, _):
        tmp[rows_at(j, MC), :] = conv(dd2, c, k2, True, j)
        return 0

    lax.fori_loop(0, px // MC, body, 0)
    step()
    turn(act2, side)
    swap_d2.wait()

    def kernel_grad(dd, pay):
        def body(j, _):
            d = dd[c, pad_at(j, MC), :].astype(F32)
            mid = dd[oc, pad_at(j, MC), pl.ds(aligned(LANES * c, LANES), LANES)].astype(F32)
            none = jnp.zeros((MC, LANES), F32)
            d = d + jnp.where(first, jnp.concatenate([none, mid], axis=1), jnp.concatenate([mid, none], axis=1))
            at = pad_at(j, MC)
            dm[0, at, :] = (pltpu.roll(d, MC - 1, 0) * not_last).astype(BF)
            dm[1, at, :] = d.astype(BF)
            dm[2, at, :] = (pltpu.roll(d, 1, 0) * not_first).astype(BF)
            return 0

        lax.fori_loop(0, px // MC, body, 0)
        hc = chans // 2

        def body(tap, _):
            a = tap // 3
            b = tap % 3
            o = dot(act_t[...], dm[b, pl.ds(aligned(side * (2 - a), 32), px), :])
            lo, hi = o[:, :LANES], o[:, LANES:]
            main = jnp.where(first, lo, hi)
            mid = jnp.where(first, hi[:hc], lo[hc:])
            pay[pl.ds(aligned(tap * chans, LANES), chans), :] = main.astype(BF)
            pay[pl.ds(aligned(9 * chans + tap * hc, HEAD_DIM), hc), :] = mid.astype(BF)
            return 0

        lax.fori_loop(0, 9, body, 0)

    kernel_grad(dd2, pay2)
    running.extend(flows(pay2, rb2, out2))
    step()

    def body(j, carry):
        at = rows_at(j, MC)
        pre = cv[at, :] * mul2 + add2
        sg = sigmoid(pre)
        u = (tmp[at, :] + conv(dd2, oc, k2, True, j)) * (sg * (1.0 + pre * (1.0 - sg)))
        tmp[at, :] = u
        return back_sums(carry, u, (cv[at, :] - mean2) * rstd2)

    s0, s1 = lax.fori_loop(0, px // MC, body, (zero8, zero8))
    t0, t1 = total(s0), total(s1)
    vx[pl.ds(9, 1), win] = (gain2 * t1 + shift2 * t0) * own_f
    vx[pl.ds(10, 1), win] = t0 * own_f
    vx[pl.ds(3, 1), win] = scale2 * t1 * own_f
    vx[pl.ds(4, 1), win] = scale2 * t0 * own_f
    gain2s = gain2 * scale2
    sp_a, sp_b = spread_of(s0, s1, gain2s)

    def body(j, carry):
        at = rows_at(j, RC)
        normed = (cv[at, :] - mean2) * rstd2
        d = rstd2 * (tmp[at, :] * gain2s - mask2(j) * (sp_a + normed * sp_b))
        low = (d * own_f).astype(BF)
        dd1[c, pad_at(j, RC), :] = low
        return carry + fold(low.astype(F32))

    vx[pl.ds(2, 1), win] = total(lax.fori_loop(0, px // RC, body, zero8))
    swap_d1 = swap(dd1.at[c, inner], dd1.at[c, inner], 8)
    step()

    def body(j, _):
        tmp[rows_at(j, MC), :] = conv(dd1, c, k1, True, j)
        return 0

    lax.fori_loop(0, px // MC, body, 0)
    step()
    turn(act1, side)
    swap_d1.wait()
    kernel_grad(dd1, pay1)
    running.extend(flows(pay1, rb1, out1))
    step()

    def body(j, carry):
        at = rows_at(j, MC)
        x = xw[at, :].astype(F32)
        pre = x * mul1 + add1
        sg = sigmoid(pre)
        u = (tmp[at, :] + conv(dd1, oc, k1, True, j)) * (sg * (1.0 + pre * (1.0 - sg)))
        tmp[at, :] = u
        return back_sums(carry, u, (x - mean1) * rstd1)

    s0, s1 = lax.fori_loop(0, px // MC, body, (zero8, zero8))
    vx[pl.ds(0, 1), win] = total(s1) * own_f
    vx[pl.ds(1, 1), win] = total(s0) * own_f
    step()

    g_sum = jnp.zeros((8, chans), F32)

    def body(j, carry):
        return carry + fold(gf[rows_at(j, RC), :].astype(F32))

    g_sum = total(lax.fori_loop(0, px // RC, body, g_sum))
    vx[pl.ds(8, 1), :] = jnp.where(first, g_sum, 0.0)
    for k in range(2):
        vx[pl.ds(11 + k, 1), :] = jnp.where(first, t_act[:, pl.ds(k * chans, chans)], 0.0)
    swap_v = swap(vx, vr, 9)

    sp_a, sp_b = spread_of(s0, s1, gain1)

    def body(j, _):
        at = rows_at(j, RC)
        normed = (xw[at, :].astype(F32) - mean1) * rstd1
        d = resid[at, :] + rstd1 * (tmp[at, :] * gain1 - mask2(j) * (sp_a + normed * sp_b))
        tmp[at, :] = d * own_f
        datt_s[at, :] = (d * own_f).astype(BF)
        return 0

    lax.fori_loop(0, px // RC, body, 0)
    swap_i = swap(datt_s.at[other_rows], ing_r, 10)
    step()

    swap_v.wait()
    vall[img] = vx[...] + vr[...]

    class Gather:
        def __init__(self):
            self.k = -1

        def advance(self):
            if self.k >= 0 and self.cp is not None:
                self.cp.wait()
                self.cp = None
            self.k += 1
            if self.k < nbits:
                bit = bits[self.k]
                at = vall.at[pl.ds((img // bit) * bit, bit)]
                base = used[0] + self.k
                self.cp = pltpu.make_async_remote_copy(
                    src_ref=at, dst_ref=at, send_sem=fs.at[base], recv_sem=fr.at[base],
                    device_id=(img + bit * (1 - 2 * ((img // bit) % 2)), c), device_id_type=MESH,
                )
                self.cp.start()
            else:
                self.cp = None

    running.append(Gather())

    swap_t.wait()
    res_out[...] = (tsum[my_rows, :] + trecv[...] + p_oo[...].reshape(1, -1)).astype(BF)
    step()
    swap_i.wait()
    tsum[pl.ds(0, half), :] = jnp.zeros((half, chans), F32)
    tsum[pl.ds(0, half), win] = tmp[my_rows, :]
    tsum[pl.ds(0, half), owin] += ing_r[...].astype(F32)
    ing_out[...] = tsum[pl.ds(0, half), :].astype(BF)

    for _ in range(2 * nbits + 2):
        step()
    for flow in running:
        if isinstance(flow, Flow):
            flow.wait_forward()
    outs = []
    for k, (src, dst) in enumerate(((out1, pk1_o), (out2, pk2_o), (outp, pp_o), (vall, vec_o))):
        cp = pltpu.make_async_copy(src, dst, lsem.at[k])
        cp.start()
        outs.append(cp)
    for cp in outs:
        cp.wait()


def finish_kernel(dims, pk1, pk2, pp, vec, *outs):
    chans, n_img, heads = dims
    (g1, s1, k1o, o1, ewo, eoo, g2, s2, k2o, o2, g3, s3, pio, oio, poo, ooo) = outs
    hc = chans // 2
    own = chans // 2

    for pay, out in ((pk1, k1o), (pk2, k2o)):

        def body(tap, _, pay=pay, out=out):
            at = pl.ds(pl.multiple_of(tap * chans, LANES), chans)
            out[at, pl.ds(0, LANES)] = pay[0, at, :].astype(F32)
            out[at, pl.ds(2 * LANES, LANES)] = pay[1, at, :].astype(F32)
            for s in range(2):
                src = pl.ds(pl.multiple_of(9 * chans + tap * hc, HEAD_DIM), hc)
                dst = pl.ds(pl.multiple_of(tap * chans + s * hc, HEAD_DIM), hc)
                out[dst, pl.ds(LANES, LANES)] = pay[s, src, :].astype(F32)
            return 0

        lax.fori_loop(0, 9, body, 0)

    width = 3 * heads * HEAD_DIM
    low = lax.broadcasted_iota(jnp.int32, (1, LANES), 1) < HEAD_DIM
    pairs = 3 * heads // 2
    for s in range(2):
        blocks = [pp[s, pl.ds(k * chans, chans), :].astype(F32) for k in range(pairs)]
        if (3 * heads) % 2:
            last = pp[s, pl.ds(pairs * chans, chans // 2), :].astype(F32)
            blocks.append(jnp.concatenate([last, pltpu.roll(last, HEAD_DIM, 1)], axis=0))
        if s == 0:
            first = blocks
        else:
            second = blocks
    cols = []
    if (3 * heads) % 2:
        cols = first[:-1]
        turned = [pltpu.roll(b, HEAD_DIM, 1) for b in second]
        cols.append(jnp.where(low, first[-1], turned[0]))
        for k in range(pairs):
            cols.append(jnp.where(low, turned[k], turned[k + 1]))
    else:
        cols = first + second
    for k, b in enumerate(cols):
        pio[:, pl.ds(k * LANES, LANES)] = b
    base = pairs * chans + ((3 * heads) % 2) * (chans // 2)
    for s in range(2):
        for b in range(chans // LANES):
            poo[pl.ds(s * own, own), pl.ds(b * LANES, LANES)] = pp[s, pl.ds(base + b * own, own), :].astype(F32)

    all_rows = vec[...]
    sums = jnp.sum(all_rows, axis=0)
    for out, k in ((g1, 0), (s1, 1), (o1, 2), (g2, 3), (s2, 4), (o2, 5), (g3, 6), (s3, 7), (ooo, 8)):
        out[...] = sums[k]
    for out, k in ((eoo, 9), (oio, 13)):
        out[pl.ds(0, chans)] = sums[k]
        out[pl.ds(chans, chans)] = sums[k + 1]
    for a in range(2):
        for b in range(2):
            ewo[pl.ds(a * chans, chans), pl.ds(b * chans, chans)] = lax.dot_general(
                vec[:, 11 + a, :], vec[:, 9 + b, :], (((0,), (0,)), ((), ())),
                preferred_element_type=F32, precision=lax.Precision.HIGHEST,
            )


def time_features(timesteps, width):
    half_width = width // 2
    frequency = jnp.exp(-math.log(10000.0) * jnp.arange(half_width, dtype=jnp.float32) / half_width)
    angles = timesteps.astype(jnp.float32)[:, None] * frequency[None, :]
    return jnp.concatenate([jnp.cos(angles), jnp.sin(angles)], axis=1)


def local(
    n_img,
    images_in, extents, timesteps, gain_first, shift_first, kernel_first, offset_first, embed_weight, embed_offset,
    gain_second, shift_second, kernel_second, offset_second, gain_attend, shift_attend, project_in, offset_in,
    project_out, offset_out, out_grad,
):
    _, stripe_rows, side, chans = images_in.shape
    px = side * side
    half = stripe_rows * side
    te = embed_weight.shape[0]
    own = chans // 2
    heads = own // HEAD_DIM
    taps = 9
    unit = 16 * n_img
    real_k = taps * chans + taps * (chans // 2)
    real_p = 3 * heads * HEAD_DIM * chans // LANES + own * (chans // LANES)
    rows_k = cdiv(real_k, unit) * unit
    rows_p = cdiv(real_p, unit) * unit
    bits = []
    while 2 ** len(bits) < n_img:
        bits.append(2 ** len(bits))
    nbits = len(bits)

    t_act = jax.nn.silu(time_features(timesteps, te))
    vm = pl.BlockSpec(memory_space=pltpu.VMEM)
    anym = pl.BlockSpec(memory_space=pl.ANY)
    smem = pl.BlockSpec(memory_space=pltpu.SMEM)
    sds = jax.ShapeDtypeStruct
    V = pltpu.VMEM
    padded = px + 2 * side
    wide = 3 * heads * LANES
    n_sem = 3 * 2 * (2 * nbits + 2) + nbits
    scratch = [
        V((taps * chans, chans), BF), V((taps * chans, chans), BF),
        V((chans + WIN - own, chans), BF), V((te, 2 * chans), BF), V((chans, wide), BF),
        V((px, WIN), BF), V((px, chans), BF), V((px, LANES), F32), V((1, 2 * chans), F32),
        V((2, padded, WIN), BF), V((2, padded, WIN), BF), V((2, px, WIN), BF), V((2, padded, WIN), BF), V((2, padded, WIN), BF),
        V((px, WIN), F32), V((px, WIN), F32), V((px, WIN), F32), V((px, WIN), F32),
        V((heads, px, LANES), BF), V((heads, px, LANES), BF), V((heads, px, LANES), BF),
        V((heads, LANES, px), BF), V((heads, LANES, px), BF), V((heads, LANES, px), BF), V((WIN, px), BF),
        V((heads, px, LANES), F32), V((heads, px, LANES), F32), V((heads, LANES, px), F32), V((px, wide), BF),
        V((px, chans), F32), V((half, chans), F32), V((px, WIN), BF), V((px, WIN), BF),
        V((3, padded, WIN), BF), V((chans, px), BF), V((half, WIN), BF),
        V((rows_k, LANES), BF), V((rows_k, LANES), BF), V((rows_p, LANES), BF),
        V((rows_k, LANES), BF), V((rows_k, LANES), BF), V((rows_p, LANES), BF),
        V((2, rows_k, LANES), BF), V((2, rows_k, LANES), BF), V((2, rows_p, LANES), BF),
        V((16, chans), F32), V((16, chans), F32), V((n_img, 16, chans), F32),
        pltpu.SemaphoreType.DMA((5,)), pltpu.SemaphoreType.DMA((11,)), pltpu.SemaphoreType.DMA((11,)),
        pltpu.SemaphoreType.DMA((n_sem,)), pltpu.SemaphoreType.DMA((n_sem,)),
    ]
    res, ing, pk1, pk2, pp, vec = pl.pallas_call(
        functools.partial(block_kernel, (side, chans, n_img, real_k, real_p, tuple(bits))),
        out_shape=(
            sds((half, chans), BF), sds((half, chans), BF), sds((2, rows_k, LANES), BF), sds((2, rows_k, LANES), BF),
            sds((2, rows_p, LANES), BF), sds((n_img, 16, chans), F32),
        ),
        in_specs=[vm, vm, smem] + [vm] * 12 + [anym, anym, anym, anym, anym],
        out_specs=(vm, vm, anym, anym, anym, anym),
        scratch_shapes=scratch,
        compiler_params=pltpu.CompilerParams(collective_id=0, has_side_effects=True, vmem_limit_bytes=60 * 2**20),
        cost_estimate=pl.CostEstimate(flops=2 * 10**10, bytes_accessed=2 * 10**7, transcendentals=4 * 10**6),
        name="block",
    )(
        images_in.reshape(half, chans), out_grad.reshape(half, chans), extents, gain_first, shift_first, offset_first,
        gain_second, shift_second, offset_second, gain_attend, shift_attend, offset_out, t_act, embed_offset, offset_in,
        kernel_first.reshape(taps * chans, chans), kernel_second.reshape(taps * chans, chans),
        project_in, project_out, embed_weight,
    )

    row = sds((chans,), F32)
    row2 = sds((2 * chans,), F32)
    kern = sds((taps * chans, chans), F32)
    outs = pl.pallas_call(
        functools.partial(finish_kernel, (chans, n_img, heads)),
        out_shape=(
            row, row, kern, row, sds((te, 2 * chans), F32), row2, row, row, kern, row, row, row,
            sds((chans, 3 * chans), F32), row2, sds((chans, chans), F32), row,
        ),
        in_specs=[vm] * 4,
        out_specs=(vm,) * 16,
        compiler_params=pltpu.CompilerParams(vmem_limit_bytes=60 * 2**20),
        name="finish",
    )(pk1, pk2, pp, vec)
    shapes = (
        gain_first, shift_first, kernel_first, offset_first, embed_weight, embed_offset, gain_second, shift_second,
        kernel_second, offset_second, gain_attend, shift_attend, project_in, offset_in, project_out, offset_out,
    )
    outs = [o.reshape(s.shape) for o, s in zip(outs, shapes)]
    return (res.reshape(images_in.shape), ing.reshape(images_in.shape), *outs)


def solution(mesh):
    n_img = mesh.shape["img"]
    stripe = P("img", "pix", None, None)
    in_specs = (stripe, P("img", None), P("img")) + (P(),) * 16 + (stripe,)
    out_specs = (stripe, stripe) + (P(),) * 16
    return jax.shard_map(
        functools.partial(local, n_img), mesh=mesh, in_specs=in_specs, out_specs=out_specs, check_vma=False
    )
```

```python
import functools
import math

import jax
import jax.numpy as jnp
from jax import lax
from jax.experimental import pallas as pl
from jax.experimental.pallas import tpu as pltpu
from jax.sharding import PartitionSpec as P

HEAD_DIM = 64
GROUPS = 32
EPSILON = 1e-05
MASKED = -1e30
BF = jnp.bfloat16
F32 = jnp.float32
MESH = pl.DeviceIdType.MESH
WIN = 256
LANES = 128
RC = 128
MC = 512
TC = 256
KERNEL_FLOWS = ((0, 4), (1, 4), (2, 3), (0, 4), (1, 3), (2, 3))
PROJECT_FLOWS = ((0, 3), (1, 3), (2, 3))
PLAN = (
    (0,),
    (2, 1),
    (3, 4, 5, 0),
    (2, 1),
    (4, 3, 5, 0),
    (13, 12),
    (2, 14, 1),
    (8, 6, 7, 4, 5, 3, 0, 12),
    (13, 2, 9, 10, 1, 14, 11, 8, 6, 7),
    (4, 5, 12),
    (3, 13, 0, 10, 9, 11, 14, 6, 2, 7, 8, 1),
    (4, 5, 10, 12, 11, 0, 2, 9, 1, 3, 4, 13, 5, 14, 6, 0, 7, 2, 8, 10, 1, 12, 3, 5, 11, 9, 4, 13, 14, 6, 0, 7, 8, 2, 13)
    + (10, 1, 11, 12, 3, 9, 7, 5, 10, 4, 14, 6, 8, 11, 13, 9, 12, 3, 7, 14, 6, 10, 8, 11, 13, 9, 12, 14, 8, 7, 6, 11, 10, 9),
)


def dot(a, b):
    return jnp.dot(a, b, preferred_element_type=F32)


def dot_nt(a, b):
    return lax.dot_general(a, b, (((1,), (1,)), ((), ())), preferred_element_type=F32)


def dot_hi(a, b):
    return jnp.dot(a, b, preferred_element_type=F32, precision=lax.Precision.HIGHEST)


def fold(v):
    return jnp.sum(v.reshape(v.shape[0] // 8, 8, v.shape[1]), axis=0)


def sigmoid(v):
    return 1.0 / (1.0 + jnp.exp(-v))


def cdiv(a, b):
    return -(-a // b)


def xor(img, bits, d):
    for pos, bit in enumerate(bits):
        if (d >> pos) & 1:
            img = img + bit * (1 - 2 * ((img // bit) % 2))
    return img


def index_in(img, bits, d=0):
    v = 0
    for pos, bit in enumerate(bits):
        mine = (img // bit) % 2
        v = v + ((1 - mine) if (d >> pos) & 1 else mine) * (1 << pos)
    return v


def shares(total, flows):
    weight = sum(w for _, w in flows)
    ends = [0]
    for k in range(len(flows)):
        ends.append(-(-total * sum(w for _, w in flows[: k + 1]) // weight))
    return [b - a for a, b in zip(ends, ends[1:])]


class Flow:
    def __init__(self, pay, rbuf, out, base, rows, stages, sems, core, img):
        self.pay, self.rbuf, self.out, self.lo, self.size = pay, rbuf, out, base, rows
        self.base, self.rows = base, rows
        self.rbase, self.stages, self.sems, self.core, self.img = base, stages, sems, core, img
        self.k = -1
        self.used = 0
        self.copies = []
        self.forwards = []

    def send(self, src, dst, device):
        send, recv, first = self.sems
        cp = pltpu.make_async_remote_copy(
            src_ref=src, dst_ref=dst, send_sem=send.at[first + self.used], recv_sem=recv.at[first + self.used],
            device_id=device, device_id_type=MESH,
        )
        self.used += 1
        cp.start()
        return cp

    def forward(self, lo, size):
        ref = self.out.at[self.core, pl.ds(pl.multiple_of(lo, 16), size)]
        self.forwards.append(self.send(ref, ref, (self.img, 1 - self.core)))

    def start(self):
        n = len(self.stages)
        self.copies = []
        if self.k < n:
            bits = self.stages[self.k]
            part = self.size >> len(bits)
            for d in range(1, 1 << len(bits)):
                lo = pl.multiple_of(self.lo + index_in(self.img, bits, d) * part, 16)
                src = self.pay.at[pl.ds(lo, part)]
                dst = self.rbuf.at[pl.ds(self.rbase + (d - 1) * part, part)]
                self.copies.append(self.send(src, dst, (xor(self.img, bits, d), self.core)))
        else:
            bits = self.stages[2 * n - 1 - self.k]
            ref = self.out.at[self.core, pl.ds(self.lo, self.size)]
            for d in range(1, 1 << len(bits)):
                self.copies.append(self.send(ref, ref, (xor(self.img, bits, d), self.core)))
            if self.k == 2 * n - 1:
                self.forward(self.lo, self.size)

    def finish(self):
        n = len(self.stages)
        for cp in self.copies:
            cp.wait()
        if self.k < n:
            bits = self.stages[self.k]
            more = (1 << len(bits)) - 1
            part = self.size >> len(bits)
            keep = pl.multiple_of(self.lo + index_in(self.img, bits) * part, 16)
            rbase = self.rbase
            step = 16
            for cand in (512, 448, 256, 128, 112, 64, 48, 32):
                if part % cand == 0:
                    step = cand
                    break

            def add(j, _):
                at = pl.ds(pl.multiple_of(keep + j * step, 16), step)
                v = self.pay[at, :].astype(F32)
                for d in range(more):
                    v = v + self.rbuf[pl.ds(pl.multiple_of(rbase + d * part + j * step, 16), step), :].astype(F32)
                if self.k == n - 1:
                    self.out[self.core, at, :] = v.astype(BF)
                else:
                    self.pay[at, :] = v.astype(BF)
                return 0

            lax.fori_loop(0, part // step, add, 0)
            self.lo, self.size = keep, part
            self.rbase += more * part
        else:
            bits = self.stages[2 * n - 1 - self.k]
            mine = index_in(self.img, bits)
            whole = pl.multiple_of(self.lo - mine * self.size, 16)
            if self.k == 2 * n - 1:
                for d in range(1, 1 << len(bits)):
                    self.forward(whole + index_in(self.img, bits, d) * self.size, self.size)
            self.lo = whole
            self.size <<= len(bits)

    def ended(self):
        return self.k >= 2 * len(self.stages)

    def advance(self):
        last = 2 * len(self.stages)
        if self.ended():
            return
        if self.k >= 0:
            self.finish()
        self.k += 1
        if self.k < last:
            self.start()


def block_kernel(dims, *refs):
    side, chans, n_img, real_k, real_p, bits, flow_sems = dims
    (
        x_in, g_in, ext, p_g1, p_s1, p_o1, p_g2, p_s2, p_o2, p_g3, p_s3, p_oo, t_act, e_off, off_in, k1_h, k2_h, wi_h, wo_h, ew_h,
        res_out, ing_out, pk1_o, pk2_o, pp_o, vec_o,
        k1, k2, wo, ew, wq, xw, gf, mask, film, act1, act2, act3, dd2, dd1,
        cv, hid, tmp, resid, qa, ka, va, kat, vat, dot_t, att_t, dqkv,
        tsum, trecv, datt_s, datt_r, dm, act_t1, act_t2, act_t3, ing_r, tsum_i,
        pay1, pay2, payp, rb1, rb2, rbp, out1, out2, outp, vx, vr, vall,
        lsem, os, xs, xr, fs, fr,
    ) = refs
    img = lax.axis_index("img")
    c = lax.axis_index("pix")
    oc = 1 - c
    px = side * side
    half = px // 2
    own_chans = chans // 2
    heads = own_chans // HEAD_DIM
    first = c == 0
    nbits = len(bits)

    def aligned(v, m):
        return pl.multiple_of(v, m)

    def rows_at(j, size):
        return pl.ds(aligned(j * size, size), size)

    def pad_at(j, size, shift=side):
        return pl.ds(aligned(j * size + shift, 32), size)

    win = pl.ds(aligned(LANES * c, LANES), WIN)
    owin = pl.ds(aligned(LANES * oc, LANES), WIN)

    barrier = pltpu.get_barrier_semaphore()
    peers = [(img, oc)]
    turns = []
    for r in range(3):
        near = list(bits[:3])[r:] + list(bits[:3])[:r]
        turns.append([[bit] for bit in near + list(bits[3:])])
    for bit in bits:
        peers.append((xor(img, [bit], 1), c))
    for peer in peers:
        pl.semaphore_signal(barrier, inc=1, device_id=peer, device_id_type=MESH)

    loads = []
    my_rows = pl.ds(aligned(half * c, half), half)
    other_rows = pl.ds(aligned(half * oc, half), half)
    copies = (
        (x_in.at[:, win], xw.at[my_rows]),
        (k1_h, k1),
        (g_in, gf.at[my_rows]),
        (ew_h, ew),
        (wi_h, dqkv.at[pl.ds(0, chans)]),
        (wo_h, wo.at[pl.ds(0, chans)]),
        (k2_h, k2),
    )
    for k, (src, dst) in enumerate(copies):
        cp = pltpu.make_async_copy(src, dst, lsem.at[k])
        cp.start()
        loads.append(cp)
    load_x, load_k1, load_g, load_ew, load_wi, load_wo, load_k2 = loads
    pl.semaphore_wait(barrier, len(peers))

    def swap(src, dst, k):
        cp = pltpu.make_async_remote_copy(
            src_ref=src, dst_ref=dst, send_sem=xs.at[k], recv_sem=xr.at[k], device_id=(img, oc), device_id_type=MESH
        )
        cp.start()
        return cp

    swap_x = swap(x_in.at[:, owin], xw.at[my_rows], 0)
    swap_g = swap(g_in, gf.at[my_rows], 1)

    lane = lax.broadcasted_iota(jnp.int32, (1, WIN), 1)
    own_f = (jnp.where(first, lane, WIN - 1 - lane) < own_chans).astype(F32)
    rows_e = ext[0, 0]
    cols_e = ext[0, 1]
    per = chans // GROUPS
    inv_entries = 1.0 / jnp.full((1, WIN), rows_e * cols_e * per, jnp.int32).astype(F32)
    gi = lax.broadcasted_iota(jnp.int32, (WIN, WIN), 0) + LANES * c
    gj = lax.broadcasted_iota(jnp.int32, (WIN, WIN), 1) + LANES * c
    same = (gi // per == gj // per).astype(F32)

    def pvec(ref):
        return ref[win].reshape(1, WIN)

    gain1, shift1, offset1 = pvec(p_g1), pvec(p_s1), pvec(p_o1)
    gain2, shift2, offset2 = pvec(p_g2), pvec(p_s2), pvec(p_o2)
    gain3, shift3 = pvec(p_g3), pvec(p_s3)

    def group_totals(a, b):
        both = dot_hi(jnp.concatenate([a, b], axis=0), same)
        return jnp.sum(both[:8], axis=0, keepdims=True), jnp.sum(both[8:], axis=0, keepdims=True)

    def total(a):
        return jnp.sum(a, axis=0, keepdims=True)

    zero8 = jnp.zeros((8, WIN), F32)

    def fill_mask(j, _):
        p = lax.broadcasted_iota(jnp.int32, (RC, LANES), 0) + j * RC
        ok = (p // side < rows_e) & (p % side < cols_e)
        mask[rows_at(j, RC), :] = ok.astype(F32)
        return 0

    lax.fori_loop(0, px // RC, fill_mask, 0)

    def mask2(j, size=RC):
        m = mask[rows_at(j, size), :]
        return jnp.concatenate([m, m], axis=1)

    edge = jnp.zeros((side, WIN), BF)
    for buf in (act1, act2, dd2, dd1):
        for s in range(2):
            buf[s, pl.ds(0, side), :] = edge
            buf[s, pl.ds(side + px, side), :] = edge
    for b in range(3):
        dm[b, pl.ds(0, side), :] = edge
        dm[b, pl.ds(side + px, side), :] = edge
    for pay, real in ((pay1, real_k), (pay2, real_k), (payp, real_p)):
        rest = pay.shape[0] - real
        if rest:
            pay[pl.ds(real, rest), :] = jnp.zeros((rest, LANES), BF)
    wo[pl.ds(chans, WIN - own_chans), :] = jnp.zeros((WIN - own_chans, chans), BF)
    for h in range(heads):
        dot_t[h, pl.ds(HEAD_DIM, HEAD_DIM), :] = jnp.zeros((HEAD_DIM, px), BF)
    att_t[pl.ds(own_chans, WIN - own_chans), :] = jnp.zeros((WIN - own_chans, px), BF)
    vx[...] = jnp.zeros(vx.shape, F32)

    def stats_step(v, m, carry):
        vm = v * m
        return carry[0] + fold(vm), carry[1] + fold(vm * v)

    def moments(carry):
        s, q = group_totals(*carry)
        mean = s * inv_entries
        return mean, lax.rsqrt(q * inv_entries - mean * mean + EPSILON)

    def body(j, carry, at=0):
        j = j + at
        return stats_step(xw[rows_at(j, RC), :].astype(F32), mask2(j), carry)

    steps = half // RC
    load_x.wait()
    carry = lax.fori_loop(0, steps, functools.partial(body, at=steps * c), (zero8, zero8))
    swap_x.wait()
    mean1, rstd1 = moments(lax.fori_loop(0, steps, functools.partial(body, at=steps * oc), carry))
    mul1 = rstd1 * gain1
    add1 = shift1 - mean1 * mul1

    def body(j, _):
        pre = xw[rows_at(j, RC), :].astype(F32) * mul1 + add1
        act1[c, pad_at(j, RC), :] = (pre * sigmoid(pre) * own_f).astype(BF)
        return 0

    lax.fori_loop(0, px // RC, body, 0)
    inner = pl.ds(side, px)
    swap_a1 = swap(act1.at[c, inner], act1.at[c, inner], 2)

    col = lax.broadcasted_iota(jnp.int32, (MC, WIN), 0) % side
    not_first = (col != 0).astype(F32)
    not_last = (col != side - 1).astype(F32)

    def conv(acts, s, kern, back, j):
        accs = []
        for b in range(3):
            acc = None
            for a in range(3):
                lhs = acts[s, pl.ds(aligned(j * MC + side * a, 32), MC), :]
                if back:
                    tap = (2 - a) * 3 + 2 - b
                    rhs = kern[pl.ds(aligned(tap * chans + LANES * c, LANES), WIN), pl.ds(aligned(LANES * s, LANES), WIN)]
                    o = dot_nt(lhs, rhs)
                else:
                    tap = a * 3 + b
                    rhs = kern[pl.ds(aligned(tap * chans + LANES * s, LANES), WIN), win]
                    o = dot(lhs, rhs)
                acc = o if acc is None else acc + o
            accs.append(acc)
        return accs[1] + pltpu.roll(accs[0], 1, 0) * not_first + pltpu.roll(accs[2], MC - 1, 0) * not_last

    def turn(acts, shift, dst):
        def body(j, _):
            a0 = acts[0, pad_at(j, TC, shift), :].astype(F32)
            a1 = acts[1, pad_at(j, TC, shift), :].astype(F32)
            at = rows_at(j, TC)
            dst[pl.ds(0, LANES), at] = a0[:, :LANES].T.astype(BF)
            dst[pl.ds(LANES, LANES), at] = (a0[:, LANES:] + a1[:, :LANES]).T.astype(BF)
            dst[pl.ds(2 * LANES, LANES), at] = a1[:, LANES:].T.astype(BF)
            return 0

        lax.fori_loop(0, px // TC, body, 0)

    load_k1.wait()

    def body(j, _):
        cv[rows_at(j, MC), :] = conv(act1, c, k1, False, j)
        return 0

    lax.fori_loop(0, px // MC, body, 0)
    lane1 = lax.broadcasted_iota(jnp.int32, (1, LANES), 1)
    low1 = lane1 < HEAD_DIM
    load_wi.wait()
    for k in range(3 * heads):
        place = 3 * heads * c + k
        blk = dqkv[pl.ds(0, chans), pl.ds(aligned((place // 2) * LANES, LANES), LANES)].astype(F32)
        blk = jnp.where(place % 2 == 0, blk, pltpu.roll(blk, HEAD_DIM, 1))
        wq[:, pl.ds(k * LANES, LANES)] = jnp.where(low1, blk, 0.0).astype(BF)

    load_ew.wait()
    t = t_act[...]
    t_a = t.astype(BF).astype(F32)
    t_b = (t - t_a).astype(BF).astype(F32)
    row16 = lax.broadcasted_iota(jnp.int32, (16, t.shape[1]), 0)
    t_rows = jnp.where(row16 == 0, t_a, jnp.where(row16 == 1, t_b, jnp.where(row16 == 2, t - t_a - t_b, 0.0)))
    film[...] = total(dot(t_rows.astype(BF), ew[...])) + e_off[...].reshape(1, -1)
    scale2 = 1.0 + film[:, win]
    move2 = film[:, pl.ds(aligned(chans + LANES * c, LANES), WIN)]

    swap_a1.wait()

    def body(j, carry):
        v = cv[rows_at(j, MC), :] + conv(act1, oc, k1, False, j) + offset1
        cv[rows_at(j, MC), :] = v
        return stats_step(v, mask2(j, MC), carry)

    mean2, rstd2 = moments(lax.fori_loop(0, px // MC, body, (zero8, zero8)))
    mul2 = rstd2 * gain2 * scale2
    add2 = (shift2 - mean2 * rstd2 * gain2) * scale2 + move2

    def body(j, _):
        pre = cv[rows_at(j, RC), :] * mul2 + add2
        act2[c, pad_at(j, RC), :] = (pre * sigmoid(pre) * own_f).astype(BF)
        return 0

    lax.fori_loop(0, px // RC, body, 0)
    swap_a2 = swap(act2.at[c, inner], act2.at[c, inner], 3)

    load_k2.wait()

    def body(j, _):
        at = rows_at(j, MC)
        hid[at, :] = conv(act2, c, k2, False, j) + offset2 + xw[at, :].astype(F32)
        return 0

    lax.fori_loop(0, px // MC, body, 0)
    swap_a2.wait()

    def body(j, carry):
        v = hid[rows_at(j, MC), :] + conv(act2, oc, k2, False, j)
        hid[rows_at(j, MC), :] = v
        return stats_step(v, mask2(j, MC), carry)

    mean3, rstd3 = moments(lax.fori_loop(0, px // MC, body, (zero8, zero8)))
    mul3 = rstd3 * gain3
    add3 = shift3 - mean3 * mul3

    def body(j, _):
        act3[c, rows_at(j, RC), :] = ((hid[rows_at(j, RC), :] * mul3 + add3) * own_f).astype(BF)
        return 0

    lax.fori_loop(0, px // RC, body, 0)
    swap_a3 = swap(act3.at[c], act3.at[c], 4)

    biases = []
    for h in range(heads):
        blk = off_in[pl.ds(aligned(LANES * (heads * c + h), LANES), LANES)].reshape(1, LANES)
        turned = pltpu.roll(jnp.broadcast_to(blk, (8, LANES)), HEAD_DIM, 1)[:1]
        bias_q = jnp.where(low1, blk, jnp.where(lane1 == HEAD_DIM, 8.0, 0.0))
        bias_v = jnp.where(low1, turned, jnp.where(lane1 < HEAD_DIM + 2, 1.0, 0.0))
        biases.append((bias_q, bias_v))
    load_wo.wait()
    load_g.wait()
    swap_g.wait()
    wo_rows = pl.ds(aligned(own_chans * c, HEAD_DIM), own_chans)

    def body(j, _):
        o = dot_nt(wo[wo_rows, :], gf[rows_at(j, MC), :])
        for h in range(heads):
            dot_t[h, pl.ds(0, HEAD_DIM), rows_at(j, MC)] = o[HEAD_DIM * h : HEAD_DIM * (h + 1)].astype(BF)
        return 0

    lax.fori_loop(0, px // MC, body, 0)

    turn(act1, side, act_t1)
    turn(act2, side, act_t2)
    swap_a3.wait()

    def body(j, _):
        at = rows_at(j, MC)
        a0 = act3[0, at, :]
        a1 = act3[1, at, :]
        hidden_key = (mask[at, :] == 0.0) & (lane1 == HEAD_DIM)
        for h in range(heads):
            cols = pl.ds(3 * LANES * h, 3 * LANES)
            o = dot(a0, wq[pl.ds(0, WIN), cols]) + dot(a1, wq[pl.ds(LANES, WIN), cols])
            q = (o[:, :LANES] + biases[h][0]).astype(BF).astype(F32) * 0.125
            k = jnp.where(hidden_key, MASKED, o[:, LANES : 2 * LANES])
            v = o[:, 2 * LANES :] + biases[h][1]
            qa[h, at, :] = q.astype(BF)
            ka[h, at, :] = k.astype(BF)
            va[h, at, :] = v.astype(BF)
            kat[h, :, at] = k.T.astype(BF)
            vat[h, :, at] = v.T.astype(BF)
        return 0

    lax.fori_loop(0, px // MC, body, 0)

    row128 = lax.broadcasted_iota(jnp.int32, (LANES, px), 0)

    def body(h, _):
        qc = qa[h]
        scores = dot_nt(ka[h], qc)
        top = jnp.max(scores, axis=0, keepdims=True)
        e = jnp.exp(scores - top).astype(BF)
        o = dot(vat[h], e)
        inv = 1.0 / o[HEAD_DIM : HEAD_DIM + 1, :]
        o = o * inv
        att_t[pl.ds(aligned(HEAD_DIM * h, HEAD_DIM), HEAD_DIM), :] = o[:HEAD_DIM].astype(BF)
        g = dot_t[h].astype(F32)
        less = -inv * jnp.sum(g * o, axis=0, keepdims=True)
        high = less.astype(BF).astype(F32)
        g = jnp.where(row128 == HEAD_DIM, high, jnp.where(row128 == HEAD_DIM + 1, less - high, g * inv)).astype(BF)
        ds = (e.astype(F32) * dot(va[h], g)).astype(BF)
        grads = (dot(kat[h], ds).T * 0.125, dot(ds, qc), dot_nt(e, g))
        for k, d in enumerate(grads):
            dqkv[:, pl.ds(aligned((3 * h + k) * LANES, LANES), LANES)] = jnp.where(low1, d, 0.0).astype(BF)
        return 0

    lax.fori_loop(0, heads, body, 0)

    def body(j, _):
        at = rows_at(j, MC)
        datt_s[at, :] = dot_nt(dqkv[at, :], wq[owin, :]).astype(BF)
        return 0

    lax.fori_loop(0, px // MC, body, 0)
    swap_da = swap(datt_s, datt_r, 5)

    def body(j, _):
        at = rows_at(j, MC)
        tmp[at, :] = dot_nt(dqkv[at, :], wq[win, :])
        return 0

    lax.fori_loop(0, px // MC, body, 0)
    turn(act3, 0, act_t3)

    used = [0]
    flows = {}

    def flow_of(key, pay, rbuf, gathered, dst, k, base, size):
        if size:
            flow = Flow(pay, rbuf, gathered, base, size, turns[k], (fs, fr, used[0]), c, img)
            flow.dst = dst
            used[0] += flow_sems
            flows[key] = flow
            flow.advance()

    def advance(point):
        for key in PLAN[point]:
            if key in flows:
                flows[key].advance()

    stores = []

    def store(src, dst):
        cp = pltpu.make_async_copy(src, dst, os.at[len(stores)])
        cp.start()
        stores.append(cp)

    def hand_out(key):
        flow = flows.pop(key)
        for cp in flow.forwards:
            cp.wait()
        at = pl.ds(flow.base, flow.rows)
        store(flow.out.at[:, at], flow.dst.at[:, at])

    swap_da.wait()

    def back_sums(carry, u, normed):
        return carry[0] + fold(u), carry[1] + fold(u * normed)

    def body(j, carry):
        at = rows_at(j, RC)
        u = tmp[at, :] + datt_r[at, :].astype(F32)
        tmp[at, :] = u
        return back_sums(carry, u, (hid[at, :] - mean3) * rstd3)

    s0, s1 = lax.fori_loop(0, px // RC, body, (zero8, zero8))
    vx[pl.ds(6, 1), win] = total(s1) * own_f
    vx[pl.ds(7, 1), win] = total(s0) * own_f

    def spread_of(s0, s1, gain):
        a, b = group_totals(s0 * gain, s1 * gain)
        return a * inv_entries, b * inv_entries

    sp_a, sp_b = spread_of(s0, s1, gain3)

    def body(j, carry):
        at = rows_at(j, RC)
        normed = (hid[at, :] - mean3) * rstd3
        d = gf[at, win].astype(F32) + rstd3 * (tmp[at, :] * gain3 - mask2(j) * (sp_a + normed * sp_b))
        resid[at, :] = d
        low = (d * own_f).astype(BF)
        dd2[c, pad_at(j, RC), :] = low
        return carry + fold(low.astype(F32))

    vx[pl.ds(5, 1), win] = total(lax.fori_loop(0, px // RC, body, zero8))
    swap_d2 = swap(dd2.at[c, inner], dd2.at[c, inner], 7)

    def body(j, _):
        tmp[rows_at(j, MC), :] = conv(dd2, c, k2, True, j)
        return 0

    lax.fori_loop(0, px // MC, body, 0)
    swap_d2.wait()

    def shifted(dd):
        def body(j, _):
            d = dd[c, pad_at(j, TC), :].astype(F32)
            mid = dd[oc, pad_at(j, TC), pl.ds(aligned(LANES * c, LANES), LANES)].astype(F32)
            none = jnp.zeros((TC, LANES), F32)
            d = d + jnp.where(first, jnp.concatenate([none, mid], axis=1), jnp.concatenate([mid, none], axis=1))
            at = pad_at(j, TC)
            dm[0, at, :] = (pltpu.roll(d, TC - 1, 0) * not_last[:TC]).astype(BF)
            dm[1, at, :] = d.astype(BF)
            dm[2, at, :] = (pltpu.roll(d, 1, 0) * not_first[:TC]).astype(BF)
            return 0

        lax.fori_loop(0, px // TC, body, 0)

    def kernel_grad(act_t, key, pay, rbuf, gathered, dst, points):
        hc = chans // 2
        unit = 16 * n_img

        def body(tap, _):
            a = tap // 3
            b = tap % 3
            o = dot(act_t[...], dm[b, pl.ds(aligned(side * (2 - a), 32), px), :])
            lo, hi = o[:, :LANES], o[:, LANES:]
            main = jnp.where(first, lo, hi)
            mid = jnp.where(first, hi[:hc], lo[hc:])
            at = tap * (chans + hc)
            pay[pl.ds(aligned(at, HEAD_DIM), chans), :] = main.astype(BF)
            pay[pl.ds(aligned(at + chans, HEAD_DIM), hc), :] = mid.astype(BF)
            return 0

        done = 0
        base = 0
        for k, units in enumerate(shares(pay.shape[0] // unit, KERNEL_FLOWS)):
            need = min(9, cdiv(base + units * unit, chans + hc))
            if need > done:
                lax.fori_loop(done, need, body, 0)
                done = need
            flow_of(key + k, pay, rbuf, gathered, dst, KERNEL_FLOWS[k][0], base, units * unit)
            base += units * unit
            if k in points:
                advance(points[k])

    shifted(dd2)
    kernel_grad(act_t2, 0, pay2, rb2, out2, pk2_o, {})

    def body(j, carry):
        at = rows_at(j, MC)
        pre = cv[at, :] * mul2 + add2
        sg = sigmoid(pre)
        u = (tmp[at, :] + conv(dd2, oc, k2, True, j)) * (sg * (1.0 + pre * (1.0 - sg)))
        tmp[at, :] = u
        return back_sums(carry, u, (cv[at, :] - mean2) * rstd2)

    s0, s1 = lax.fori_loop(0, px // MC, body, (zero8, zero8))
    advance(0)
    t0, t1 = total(s0), total(s1)
    vx[pl.ds(9, 1), win] = (gain2 * t1 + shift2 * t0) * own_f
    vx[pl.ds(10, 1), win] = t0 * own_f
    vx[pl.ds(3, 1), win] = scale2 * t1 * own_f
    vx[pl.ds(4, 1), win] = scale2 * t0 * own_f
    gain2s = gain2 * scale2
    sp_a, sp_b = spread_of(s0, s1, gain2s)

    def body(j, carry):
        at = rows_at(j, RC)
        normed = (cv[at, :] - mean2) * rstd2
        d = rstd2 * (tmp[at, :] * gain2s - mask2(j) * (sp_a + normed * sp_b))
        low = (d * own_f).astype(BF)
        dd1[c, pad_at(j, RC), :] = low
        return carry + fold(low.astype(F32))

    vx[pl.ds(2, 1), win] = total(lax.fori_loop(0, px // RC, body, zero8))
    swap_d1 = swap(dd1.at[c, inner], dd1.at[c, inner], 8)

    advance(1)

    for k in range(3 * heads // 2):
        o = dot(act_t3[...], dqkv[:, pl.ds(2 * LANES * k, 2 * LANES)])
        pair = o[:, :LANES] + pltpu.roll(o[:, LANES:], HEAD_DIM, 1)
        payp[pl.ds(k * chans, chans), :] = pair.astype(BF)
    base = (3 * heads // 2) * chans
    if (3 * heads) % 2:
        o = dot(act_t3[...], dqkv[:, pl.ds((3 * heads - 1) * LANES, LANES)])
        pair = o[: chans // 2] + pltpu.roll(o[chans // 2 :], HEAD_DIM, 1)
        payp[pl.ds(base, chans // 2), :] = pair.astype(BF)
        base += chans // 2
    o = dot(att_t[pl.ds(0, own_chans), :], gf[...])
    for b in range(chans // LANES):
        payp[pl.ds(base + b * own_chans, own_chans), :] = o[:, b * LANES : (b + 1) * LANES].astype(BF)

    for h in range(heads):
        z = jnp.zeros((8, LANES), F32)

        def body(j, carry, h=h):
            at = rows_at(j, TC)
            q = dqkv[at, pl.ds(3 * h * LANES, LANES)].astype(F32)
            v = dqkv[at, pl.ds((3 * h + 2) * LANES, LANES)].astype(F32)
            return carry[0] + fold(q), carry[1] + fold(v)

        sum_q, sum_v = lax.fori_loop(0, px // TC, body, (z, z))
        sums = total(sum_q + pltpu.roll(sum_v, HEAD_DIM, 1))
        vx[pl.ds(13, 1), pl.ds(LANES * h, LANES)] = jnp.where(first, sums, 0.0)
        vx[pl.ds(14, 1), pl.ds(LANES * h, LANES)] = jnp.where(first, 0.0, sums)

    advance(2)
    at = 0
    for k, units in enumerate(shares(payp.shape[0] // (16 * n_img), PROJECT_FLOWS)):
        flow_of(12 + k, payp, rbp, outp, pp_o, PROJECT_FLOWS[k][0], at, units * 16 * n_img)
        at += units * 16 * n_img

    swap_d1.wait()
    shifted(dd1)
    advance(3)
    kernel_grad(act_t1, 6, pay1, rb1, out1, pk1_o, {2: 4, 3: 5, 4: 6})

    def body(j, _):
        tmp[rows_at(j, MC), :] = conv(dd1, c, k1, True, j)
        return 0

    lax.fori_loop(0, px // MC, body, 0)
    advance(7)

    def body(j, carry):
        at = rows_at(j, MC)
        x = xw[at, :].astype(F32)
        pre = x * mul1 + add1
        sg = sigmoid(pre)
        u = (tmp[at, :] + conv(dd1, oc, k1, True, j)) * (sg * (1.0 + pre * (1.0 - sg)))
        tmp[at, :] = u
        return back_sums(carry, u, (x - mean1) * rstd1)

    s0, s1 = lax.fori_loop(0, px // MC, body, (zero8, zero8))
    advance(8)
    vx[pl.ds(0, 1), win] = total(s1) * own_f
    vx[pl.ds(1, 1), win] = total(s0) * own_f

    g_sum = jnp.zeros((8, chans), F32)

    def body(j, carry):
        return carry + fold(gf[rows_at(j, RC), :].astype(F32))

    g_sum = total(lax.fori_loop(0, px // RC, body, g_sum))
    vx[pl.ds(8, 1), :] = jnp.where(first, g_sum, 0.0)
    for k in range(2):
        vx[pl.ds(11 + k, 1), :] = jnp.where(first, t_act[:, pl.ds(k * chans, chans)], 0.0)
    swap_v = swap(vx, vr, 9)

    sp_a, sp_b = spread_of(s0, s1, gain1)

    def body(j, _):
        at = rows_at(j, RC)
        normed = (xw[at, :].astype(F32) - mean1) * rstd1
        d = resid[at, :] + rstd1 * (tmp[at, :] * gain1 - mask2(j) * (sp_a + normed * sp_b))
        tmp[at, :] = d * own_f
        datt_s[at, :] = (d * own_f).astype(BF)
        return 0

    lax.fori_loop(0, px // RC, body, 0)
    swap_i = swap(datt_s.at[other_rows], ing_r, 10)

    swap_v.wait()
    vall[img] = vx[...] + vr[...]

    class Gather:
        def __init__(self):
            self.k = -1
            self.copies = []

        def advance(self):
            for cp in self.copies:
                cp.wait()
            self.copies = []
            self.k += 1
            if self.k < nbits:
                bit = bits[self.k]
                at = vall.at[pl.ds((img // bit) * bit, bit)]
                k = used[0]
                used[0] += 1
                cp = pltpu.make_async_remote_copy(
                    src_ref=at, dst_ref=at, send_sem=fs.at[k], recv_sem=fr.at[k],
                    device_id=(xor(img, [bit], 1), c), device_id_type=MESH,
                )
                cp.start()
                self.copies.append(cp)

    vectors = Gather()
    vectors.advance()
    advance(9)

    def body(j, _):
        at = rows_at(j, TC)
        tsum[at, :] = dot(att_t[:, at].astype(F32).T.astype(BF), wo[pl.ds(aligned(own_chans * c, HEAD_DIM), WIN), :])
        tsum[at, win] += hid[at, :] * own_f
        return 0

    lax.fori_loop(0, px // TC, body, 0)
    swap_t = swap(tsum.at[other_rows], trecv, 6)

    advance(10)
    vectors.advance()

    swap_i.wait()
    tsum_i[...] = jnp.zeros((half, chans), F32)
    tsum_i[:, win] = tmp[my_rows, :]
    tsum_i[:, owin] += ing_r[...].astype(F32)
    ing_out[...] = tsum_i[...].astype(BF)
    swap_t.wait()
    res_out[...] = (tsum[my_rows, :] + trecv[...] + p_oo[...].reshape(1, -1)).astype(BF)
    ended = {}
    for n, key in enumerate(PLAN[11]):
        if key in flows:
            flows[key].advance()
            if flows[key].ended():
                ended.setdefault(key, n)
        if n % 8 == 7:
            vectors.advance()
        for key in [k for k in ended if ended[k] + 6 == n]:
            hand_out(key)
    while any(not flow.ended() for flow in flows.values()):
        for flow in flows.values():
            flow.advance()
        vectors.advance()
    while vectors.copies:
        vectors.advance()
    store(vall, vec_o)
    for key in sorted(flows, key=lambda k: ended.get(k, 0)):
        hand_out(key)
    for cp in stores:
        cp.wait()


def finish_kernel(dims, pk1, pk2, pp, vec, res, ing, *refs):
    chans, heads = dims
    (res_o, ing_o, g1, s1, k1o, o1, ewo, eoo, g2, s2, k2o, o2, g3, s3, pio, oio, poo, ooo) = refs[:18]
    (b1, b2, bp, bv, br, f1, f2, fe, fi, fo, isem, osem) = refs[18:]
    hc = chans // 2
    own = chans // 2
    te = fe.shape[0]

    def move(src, dst, sem):
        cp = pltpu.make_async_copy(src, dst, sem)
        cp.start()
        return cp

    each = 3 * (chans + hc)
    get_2 = [move(pk2.at[:, pl.ds(a * each, each)], b2.at[:, pl.ds(a * each, each)], isem.at[a]) for a in range(3)]
    get_v = move(vec, bv, isem.at[3])
    get_1 = [move(pk1.at[:, pl.ds(a * each, each)], b1.at[:, pl.ds(a * each, each)], isem.at[4 + a]) for a in range(3)]
    get_p = move(pp, bp, isem.at[7])
    get_r = [move(src, br.at[k], isem.at[8 + k]) for k, src in enumerate((res, ing))]
    out = []

    def kernel(n, pay, get, full, dst):
        for a in range(3):
            get[a].wait()

            def body(b, _, a=a):
                tap = 3 * a + b
                src = tap * (chans + hc)
                at = pl.ds(pl.multiple_of(tap * chans, LANES), chans)
                main = pl.ds(pl.multiple_of(src, HEAD_DIM), chans)
                full[at, pl.ds(0, LANES)] = pay[0, main, :].astype(F32)
                full[at, pl.ds(2 * LANES, LANES)] = pay[1, main, :].astype(F32)
                mid = pl.ds(pl.multiple_of(src + chans, HEAD_DIM), hc)
                for s in range(2):
                    to = pl.ds(pl.multiple_of(tap * chans + s * hc, HEAD_DIM), hc)
                    full[to, pl.ds(LANES, LANES)] = pay[s, mid, :].astype(F32)
                return 0

            lax.fori_loop(0, 3, body, 0)
            part = pl.ds(3 * a * chans, 3 * chans)
            out.append(move(full.at[part], dst.at[part], osem.at[3 + 3 * n + a]))

    kernel(0, b2, get_2, f2, k2o)

    get_v.wait()
    sums = jnp.sum(bv[...], axis=0)
    for ref, k in ((g1, 0), (s1, 1), (o1, 2), (g2, 3), (s2, 4), (o2, 5), (g3, 6), (s3, 7), (ooo, 8)):
        ref[...] = sums[k]
    for ref, k in ((eoo, 9), (oio, 13)):
        ref[pl.ds(0, chans)] = sums[k]
        ref[pl.ds(chans, chans)] = sums[k + 1]
    for a in range(2):
        for b in range(2):
            fe[pl.ds(a * chans, chans), pl.ds(b * chans, chans)] = lax.dot_general(
                bv[:, 11 + a, :], bv[:, 9 + b, :], (((0,), (0,)), ((), ())),
                preferred_element_type=F32, precision=lax.Precision.HIGHEST,
            )
    out.append(move(fe, ewo, osem.at[2]))

    kernel(1, b1, get_1, f1, k1o)
    for k, dst in enumerate((res_o, ing_o)):
        get_r[k].wait()
        out.append(move(br.at[k], dst, osem.at[k]))

    get_p.wait()
    low = lax.broadcasted_iota(jnp.int32, (1, LANES), 1) < HEAD_DIM
    pairs = 3 * heads // 2
    odd = (3 * heads) % 2
    sides = []
    for s in range(2):
        blocks = [bp[s, pl.ds(k * chans, chans), :].astype(F32) for k in range(pairs)]
        if odd:
            last = bp[s, pl.ds(pairs * chans, chans // 2), :].astype(F32)
            blocks.append(jnp.concatenate([last, pltpu.roll(last, HEAD_DIM, 1)], axis=0))
        sides.append(blocks)
    cols = sides[0] + sides[1]
    if odd:
        turned = [pltpu.roll(b, HEAD_DIM, 1) for b in sides[1]]
        cols = sides[0][:-1] + [jnp.where(low, sides[0][-1], turned[0])]
        cols += [jnp.where(low, turned[k], turned[k + 1]) for k in range(pairs)]
    for k, b in enumerate(cols):
        fi[:, pl.ds(k * LANES, LANES)] = b
    out.append(move(fi, pio, osem.at[9]))
    base = pairs * chans + odd * (chans // 2)
    for s in range(2):
        for b in range(chans // LANES):
            fo[pl.ds(s * own, own), pl.ds(b * LANES, LANES)] = bp[s, pl.ds(base + b * own, own), :].astype(F32)
    out.append(move(fo, poo, osem.at[10]))
    for cp in out:
        cp.wait()


def time_features(timesteps, width):
    half_width = width // 2
    frequency = jnp.exp(-math.log(10000.0) * jnp.arange(half_width, dtype=jnp.float32) / half_width)
    angles = timesteps.astype(jnp.float32)[:, None] * frequency[None, :]
    return jnp.concatenate([jnp.cos(angles), jnp.sin(angles)], axis=1)


def local(
    n_img,
    images_in, extents, timesteps, gain_first, shift_first, kernel_first, offset_first, embed_weight, embed_offset,
    gain_second, shift_second, kernel_second, offset_second, gain_attend, shift_attend, project_in, offset_in,
    project_out, offset_out, out_grad,
):
    _, stripe_rows, side, chans = images_in.shape
    px = side * side
    half = stripe_rows * side
    te = embed_weight.shape[0]
    own = chans // 2
    heads = own // HEAD_DIM
    taps = 9
    unit = 16 * n_img
    real_k = taps * (chans + chans // 2)
    real_p = 3 * heads * HEAD_DIM * chans // LANES + own * (chans // LANES)
    rows_k = cdiv(real_k, unit) * unit
    rows_p = cdiv(real_p, unit) * unit
    bits = []
    while 2 ** len(bits) < n_img:
        bits.append(2 ** len(bits))
    nbits = len(bits)

    t_act = jax.nn.silu(time_features(timesteps, te))
    vm = pl.BlockSpec(memory_space=pltpu.VMEM)
    anym = pl.BlockSpec(memory_space=pl.ANY)
    smem = pl.BlockSpec(memory_space=pltpu.SMEM)
    sds = jax.ShapeDtypeStruct
    V = pltpu.VMEM
    padded = px + 2 * side
    wide = 3 * heads * LANES
    flow_sems = 2 * nbits + 2
    n_sem = (2 * len(KERNEL_FLOWS) + len(PROJECT_FLOWS)) * flow_sems + nbits
    scratch = [
        V((taps * chans, chans), BF), V((taps * chans, chans), BF),
        V((chans + WIN - own, chans), BF), V((te, 2 * chans), BF), V((chans, wide), BF),
        V((px, WIN), BF), V((px, chans), BF), V((px, LANES), F32), V((1, 2 * chans), F32),
        V((2, padded, WIN), BF), V((2, padded, WIN), BF), V((2, px, WIN), BF), V((2, padded, WIN), BF), V((2, padded, WIN), BF),
        V((px, WIN), F32), V((px, WIN), F32), V((px, WIN), F32), V((px, WIN), F32),
        V((heads, px, LANES), BF), V((heads, px, LANES), BF), V((heads, px, LANES), BF),
        V((heads, LANES, px), BF), V((heads, LANES, px), BF), V((heads, LANES, px), BF), V((WIN, px), BF), V((px, wide), BF),
        V((px, chans), F32), V((half, chans), F32), V((px, WIN), BF), V((px, WIN), BF),
        V((3, padded, WIN), BF), V((chans, px), BF), V((chans, px), BF), V((chans, px), BF), V((half, WIN), BF), V((half, chans), F32),
        V((rows_k, LANES), BF), V((rows_k, LANES), BF), V((rows_p, LANES), BF),
        V((rows_k, LANES), BF), V((rows_k, LANES), BF), V((rows_p, LANES), BF),
        V((2, rows_k, LANES), BF), V((2, rows_k, LANES), BF), V((2, rows_p, LANES), BF),
        V((16, chans), F32), V((16, chans), F32), V((n_img, 16, chans), F32),
        pltpu.SemaphoreType.DMA((7,)), pltpu.SemaphoreType.DMA((16,)), pltpu.SemaphoreType.DMA((11,)), pltpu.SemaphoreType.DMA((11,)),
        pltpu.SemaphoreType.DMA((n_sem,)), pltpu.SemaphoreType.DMA((n_sem,)),
    ]
    res, ing, pk1, pk2, pp, vec = pl.pallas_call(
        functools.partial(block_kernel, (side, chans, n_img, real_k, real_p, tuple(bits), flow_sems)),
        out_shape=(
            sds((half, chans), BF), sds((half, chans), BF), sds((2, rows_k, LANES), BF), sds((2, rows_k, LANES), BF),
            sds((2, rows_p, LANES), BF), sds((n_img, 16, chans), F32),
        ),
        in_specs=[anym, anym, smem] + [vm] * 12 + [anym, anym, anym, anym, anym],
        out_specs=(vm, vm, anym, anym, anym, anym),
        scratch_shapes=scratch,
        compiler_params=pltpu.CompilerParams(collective_id=0, has_side_effects=True, vmem_limit_bytes=60 * 2**20),
        cost_estimate=pl.CostEstimate(flops=2 * 10**10, bytes_accessed=2 * 10**7, transcendentals=4 * 10**6),
        name="block",
    )(
        images_in.reshape(half, chans), out_grad.reshape(half, chans), extents, gain_first, shift_first, offset_first,
        gain_second, shift_second, offset_second, gain_attend, shift_attend, offset_out, t_act, embed_offset, offset_in,
        kernel_first.reshape(taps * chans, chans), kernel_second.reshape(taps * chans, chans),
        project_in, project_out, embed_weight,
    )

    row = sds((chans,), F32)
    row2 = sds((2 * chans,), F32)
    kern = sds((taps * chans, chans), F32)
    stripe = sds((half, chans), BF)
    outs = pl.pallas_call(
        functools.partial(finish_kernel, (chans, heads)),
        out_shape=(
            stripe, stripe, row, row, kern, row, sds((te, 2 * chans), F32), row2, row, row, kern, row, row, row,
            sds((chans, 3 * chans), F32), row2, sds((chans, chans), F32), row,
        ),
        in_specs=[anym] * 6,
        out_specs=(anym, anym, vm, vm, anym, vm, anym, vm, vm, vm, anym, vm, vm, vm, anym, vm, anym, vm),
        scratch_shapes=[
            V((2, rows_k, LANES), BF), V((2, rows_k, LANES), BF), V((2, rows_p, LANES), BF), V((n_img, 16, chans), F32),
            V((2, half, chans), BF), V((taps * chans, chans), F32), V((taps * chans, chans), F32), V((te, 2 * chans), F32),
            V((chans, 3 * chans), F32), V((chans, chans), F32),
            pltpu.SemaphoreType.DMA((10,)), pltpu.SemaphoreType.DMA((11,)),
        ],
        compiler_params=pltpu.CompilerParams(vmem_limit_bytes=60 * 2**20),
        cost_estimate=pl.CostEstimate(flops=10**8, bytes_accessed=23 * 10**6, transcendentals=0),
        name="finish",
    )(pk1, pk2, pp, vec, res, ing)
    res, ing, *outs = outs
    shapes = (
        gain_first, shift_first, kernel_first, offset_first, embed_weight, embed_offset, gain_second, shift_second,
        kernel_second, offset_second, gain_attend, shift_attend, project_in, offset_in, project_out, offset_out,
    )
    outs = [o.reshape(s.shape) for o, s in zip(outs, shapes)]
    return (res.reshape(images_in.shape), ing.reshape(images_in.shape), *outs)


def solution(mesh):
    n_img = mesh.shape["img"]
    stripe = P("img", "pix", None, None)
    in_specs = (stripe, P("img", None), P("img")) + (P(),) * 16 + (stripe,)
    out_specs = (stripe, stripe) + (P(),) * 16
    return jax.shard_map(
        functools.partial(local, n_img), mesh=mesh, in_specs=in_specs, out_specs=out_specs, check_vma=False
    )
```

```python
import functools
import math

import jax
import jax.numpy as jnp
from jax import lax
from jax.experimental import pallas as pl
from jax.experimental.pallas import tpu as pltpu
from jax.sharding import PartitionSpec as P

HEAD_DIM = 64
GROUPS = 32
EPSILON = 1e-05
MASKED = -1e30
BF = jnp.bfloat16
F32 = jnp.float32
MESH = pl.DeviceIdType.MESH
WIN = 256
LANES = 128
RC = 256
MC = 512
TC = 256
X_FIRST, Y_FIRST, Z_FIRST = (0, 1, 2, 3), (1, 2, 0, 3), (2, 0, 1, 3)
KERNEL_FLOWS = ((X_FIRST, 4), (Y_FIRST, 4), (Z_FIRST, 4), (X_FIRST, 3), (Y_FIRST, 3), (Z_FIRST, 3))
PROJECT_FLOWS = ((X_FIRST, 3), (Y_FIRST, 3), (Z_FIRST, 3))
SECOND, FIRST, PROJECT = tuple(range(16)), tuple(range(16, 32)), tuple(range(32, 48))
PLAN = (
    (),
    SECOND,
    (),
    SECOND,
    SECOND + PROJECT,
    SECOND + FIRST + PROJECT,
    (),
    SECOND + FIRST + PROJECT,
    (),
)


def dot(a, b):
    return jnp.dot(a, b, preferred_element_type=F32)


def dot_nt(a, b):
    return lax.dot_general(a, b, (((1,), (1,)), ((), ())), preferred_element_type=F32)


def dot_hi(a, b):
    return jnp.dot(a, b, preferred_element_type=F32, precision=lax.Precision.HIGHEST)


def fold(v):
    return jnp.sum(v.reshape(v.shape[0] // 8, 8, v.shape[1]), axis=0)


def sigmoid(v):
    return 1.0 / (1.0 + jnp.exp(-v))


def cdiv(a, b):
    return -(-a // b)


def xor(img, bits, d):
    for pos, bit in enumerate(bits):
        if (d >> pos) & 1:
            img = img + bit * (1 - 2 * ((img // bit) % 2))
    return img


def index_in(img, bits, d=0):
    v = 0
    for pos, bit in enumerate(bits):
        mine = (img // bit) % 2
        v = v + ((1 - mine) if (d >> pos) & 1 else mine) * (1 << pos)
    return v


def shares(total, flows):
    weight = sum(w for _, w in flows)
    ends = [0]
    for k in range(len(flows)):
        ends.append(-(-total * sum(w for _, w in flows[: k + 1]) // weight))
    return [b - a for a, b in zip(ends, ends[1:])]


class Flow:
    def __init__(self, pay, rbuf, out, base, rows, stages, sems, core, img):
        self.pay, self.rbuf, self.out, self.lo, self.size = pay, rbuf, out, base, rows
        self.base, self.rows = base, rows
        self.rbase, self.stages, self.sems, self.core, self.img = base, stages, sems, core, img
        self.k = -1
        self.used = 0
        self.copies = []
        self.forwards = []

    def send(self, src, dst, device):
        send, recv, first = self.sems
        cp = pltpu.make_async_remote_copy(
            src_ref=src, dst_ref=dst, send_sem=send.at[first + self.used], recv_sem=recv.at[first + self.used],
            device_id=device, device_id_type=MESH,
        )
        self.used += 1
        cp.start()
        return cp

    def forward(self, lo, size):
        ref = self.out.at[self.core, pl.ds(pl.multiple_of(lo, 16), size)]
        self.forwards.append(self.send(ref, ref, (self.img, 1 - self.core)))

    def start(self):
        n = len(self.stages)
        self.copies = []
        if self.k < n:
            bits = self.stages[self.k]
            part = self.size >> len(bits)
            for d in range(1, 1 << len(bits)):
                lo = pl.multiple_of(self.lo + index_in(self.img, bits, d) * part, 16)
                src = self.pay.at[pl.ds(lo, part)]
                dst = self.rbuf.at[pl.ds(self.rbase + (d - 1) * part, part)]
                self.copies.append(self.send(src, dst, (xor(self.img, bits, d), self.core)))
        else:
            bits = self.stages[2 * n - 1 - self.k]
            ref = self.out.at[self.core, pl.ds(self.lo, self.size)]
            for d in range(1, 1 << len(bits)):
                self.copies.append(self.send(ref, ref, (xor(self.img, bits, d), self.core)))
            if self.k == 2 * n - 1:
                self.forward(self.lo, self.size)

    def finish(self):
        n = len(self.stages)
        for cp in self.copies:
            cp.wait()
        if self.k < n:
            bits = self.stages[self.k]
            more = (1 << len(bits)) - 1
            part = self.size >> len(bits)
            keep = pl.multiple_of(self.lo + index_in(self.img, bits) * part, 16)
            rbase = self.rbase
            step = 16
            for cand in (512, 448, 256, 128, 112, 64, 48, 32):
                if part % cand == 0:
                    step = cand
                    break

            def add(j, _):
                at = pl.ds(pl.multiple_of(keep + j * step, 16), step)
                v = self.pay[at, :].astype(F32)
                for d in range(more):
                    v = v + self.rbuf[pl.ds(pl.multiple_of(rbase + d * part + j * step, 16), step), :].astype(F32)
                if self.k == n - 1:
                    self.out[self.core, at, :] = v.astype(BF)
                else:
                    self.pay[at, :] = v.astype(BF)
                return 0

            lax.fori_loop(0, part // step, add, 0)
            self.lo, self.size = keep, part
            self.rbase += more * part
        else:
            bits = self.stages[2 * n - 1 - self.k]
            mine = index_in(self.img, bits)
            whole = pl.multiple_of(self.lo - mine * self.size, 16)
            if self.k == 2 * n - 1:
                for d in range(1, 1 << len(bits)):
                    self.forward(whole + index_in(self.img, bits, d) * self.size, self.size)
            self.lo = whole
            self.size <<= len(bits)

    def ended(self):
        return self.k >= 2 * len(self.stages)

    def advance(self):
        last = 2 * len(self.stages)
        if self.ended():
            return
        if self.k >= 0:
            self.finish()
        self.k += 1
        if self.k < last:
            self.start()


def block_kernel(dims, *refs):
    side, chans, n_img, real_k, real_p, bits, flow_sems = dims
    (
        x_in, g_in, ext, p_g1, p_s1, p_o1, p_g2, p_s2, p_o2, p_g3, p_s3, p_oo, t_act, e_off, off_in, k1_h, k2_h, wi_h, wo_h, ew_h,
        res_v, ing_v, out1, out2, outp, vall,
        k1, k2, wo, ew, wq, xw, gf, mask, film, act1, act2, act3, dd2, dd1,
        cv, hid, tmp, resid, qa, ka, va, kat, vat, dot_t, att_t, dqkv,
        tsum, trecv, datt_s, datt_r, dm, act_t1, act_t2, act_t3, ing_r,
        pay1, pay2, payp, rb1, rb2, rbp, vx, vr,
        lsem, xs, xr, fs, fr,
    ) = refs
    img = lax.axis_index("img")
    c = lax.axis_index("pix")
    oc = 1 - c
    px = side * side
    half = px // 2
    own_chans = chans // 2
    heads = own_chans // HEAD_DIM
    first = c == 0
    nbits = len(bits)

    def aligned(v, m):
        return pl.multiple_of(v, m)

    def rows_at(j, size):
        return pl.ds(aligned(j * size, size), size)

    def pad_at(j, size, shift=side):
        return pl.ds(aligned(j * size + shift, 32), size)

    win = pl.ds(aligned(LANES * c, LANES), WIN)
    owin = pl.ds(aligned(LANES * oc, LANES), WIN)

    barrier = pltpu.get_barrier_semaphore()
    peers = [(img, oc)]

    def stages(order):
        near = [bits[k] for k in order if k < nbits]
        return [[bit] for bit in near + list(bits[len(order) :])]

    for bit in bits:
        peers.append((xor(img, [bit], 1), c))
    for peer in peers:
        pl.semaphore_signal(barrier, inc=1, device_id=peer, device_id_type=MESH)

    loads = []
    my_rows = pl.ds(aligned(half * c, half), half)
    other_rows = pl.ds(aligned(half * oc, half), half)
    copies = (
        (x_in.at[:, win], xw.at[my_rows]),
        (k1_h, k1),
        (g_in, gf.at[my_rows]),
        (ew_h, ew),
        (wi_h, dqkv.at[pl.ds(0, chans)]),
        (wo_h, wo.at[pl.ds(0, chans)]),
        (k2_h, k2),
    )
    for k, (src, dst) in enumerate(copies):
        cp = pltpu.make_async_copy(src, dst, lsem.at[k])
        cp.start()
        loads.append(cp)
    load_x, load_k1, load_g, load_ew, load_wi, load_wo, load_k2 = loads
    pl.semaphore_wait(barrier, len(peers))

    def swap(src, dst, k):
        cp = pltpu.make_async_remote_copy(
            src_ref=src, dst_ref=dst, send_sem=xs.at[k], recv_sem=xr.at[k], device_id=(img, oc), device_id_type=MESH
        )
        cp.start()
        return cp

    swap_x = swap(x_in.at[:, owin], xw.at[my_rows], 0)
    swap_g = swap(g_in, gf.at[my_rows], 1)

    lane = lax.broadcasted_iota(jnp.int32, (1, WIN), 1)
    own_f = (jnp.where(first, lane, WIN - 1 - lane) < own_chans).astype(F32)
    rows_e = ext[0, 0]
    cols_e = ext[0, 1]
    per = chans // GROUPS
    inv_entries = 1.0 / jnp.full((1, WIN), rows_e * cols_e * per, jnp.int32).astype(F32)
    gi = lax.broadcasted_iota(jnp.int32, (WIN, WIN), 0) + LANES * c
    gj = lax.broadcasted_iota(jnp.int32, (WIN, WIN), 1) + LANES * c
    same = (gi // per == gj // per).astype(F32).astype(BF)

    def pvec(ref):
        return ref[win].reshape(1, WIN)

    gain1, shift1, offset1 = pvec(p_g1), pvec(p_s1), pvec(p_o1)
    gain2, shift2, offset2 = pvec(p_g2), pvec(p_s2), pvec(p_o2)
    gain3, shift3 = pvec(p_g3), pvec(p_s3)

    def group_totals(a, b):
        both = jnp.concatenate([a, b], axis=0)
        high = both.astype(BF)
        rest = both - high.astype(F32)
        mid = rest.astype(BF)
        low = (rest - mid.astype(F32)).astype(BF)
        o = dot(jnp.concatenate([high, mid, low], axis=0), same)
        o = o[:16] + o[16:32] + o[32:]
        return jnp.sum(o[:8], axis=0, keepdims=True), jnp.sum(o[8:], axis=0, keepdims=True)

    def total(a):
        return jnp.sum(a, axis=0, keepdims=True)

    zero8 = jnp.zeros((8, WIN), F32)

    def fill_mask(j, _):
        p = lax.broadcasted_iota(jnp.int32, (RC, LANES), 0) + j * RC
        ok = (p // side < rows_e) & (p % side < cols_e)
        mask[rows_at(j, RC), :] = ok.astype(F32)
        return 0

    lax.fori_loop(0, px // RC, fill_mask, 0)

    def mask2(j, size=RC):
        m = mask[rows_at(j, size), :]
        return jnp.concatenate([m, m], axis=1)

    edge = jnp.zeros((side, WIN), BF)
    for buf in (act1, act2, dd2, dd1):
        for s in range(2):
            buf[s, pl.ds(0, side), :] = edge
            buf[s, pl.ds(side + px, side), :] = edge
    for b in range(3):
        dm[b, pl.ds(0, side), :] = edge
        dm[b, pl.ds(side + px, side), :] = edge
    for pay, real in ((pay1, real_k), (pay2, real_k), (payp, real_p)):
        rest = pay.shape[0] - real
        if rest:
            pay[pl.ds(real, rest), :] = jnp.zeros((rest, LANES), BF)
    wo[pl.ds(chans, WIN - own_chans), :] = jnp.zeros((WIN - own_chans, chans), BF)
    for h in range(heads):
        dot_t[h, pl.ds(HEAD_DIM, HEAD_DIM), :] = jnp.zeros((HEAD_DIM, px), BF)
    att_t[pl.ds(own_chans, WIN - own_chans), :] = jnp.zeros((WIN - own_chans, px), BF)
    vx[...] = jnp.zeros(vx.shape, F32)

    def stats_step(v, m, carry):
        vm = v * m
        return carry[0] + fold(vm), carry[1] + fold(vm * v)

    def moments(carry):
        s, q = group_totals(*carry)
        mean = s * inv_entries
        return mean, lax.rsqrt(q * inv_entries - mean * mean + EPSILON)

    def body(j, carry, at=0):
        j = j + at
        return stats_step(xw[rows_at(j, RC), :].astype(F32), mask2(j), carry)

    steps = half // RC
    load_x.wait()
    carry = lax.fori_loop(0, steps, functools.partial(body, at=steps * c), (zero8, zero8))
    swap_x.wait()
    mean1, rstd1 = moments(lax.fori_loop(0, steps, functools.partial(body, at=steps * oc), carry))
    mul1 = rstd1 * gain1
    add1 = shift1 - mean1 * mul1

    def body(j, _):
        pre = xw[rows_at(j, RC), :].astype(F32) * mul1 + add1
        act1[c, pad_at(j, RC), :] = (pre * sigmoid(pre) * own_f).astype(BF)
        return 0

    lax.fori_loop(0, px // RC, body, 0)
    inner = pl.ds(side, px)
    swap_a1 = swap(act1.at[c, inner], act1.at[c, inner], 2)

    col = lax.broadcasted_iota(jnp.int32, (MC, WIN), 0) % side
    not_first = (col != 0).astype(F32)
    not_last = (col != side - 1).astype(F32)

    def conv(acts, s, kern, back, j):
        accs = []
        for b in range(3):
            acc = None
            for a in range(3):
                lhs = acts[s, pl.ds(aligned(j * MC + side * a, 32), MC), :]
                if back:
                    tap = (2 - a) * 3 + 2 - b
                    rhs = kern[pl.ds(aligned(tap * chans + LANES * c, LANES), WIN), pl.ds(aligned(LANES * s, LANES), WIN)]
                    o = dot_nt(lhs, rhs)
                else:
                    tap = a * 3 + b
                    rhs = kern[pl.ds(aligned(tap * chans + LANES * s, LANES), WIN), win]
                    o = dot(lhs, rhs)
                acc = o if acc is None else acc + o
            accs.append(acc)
        return accs[1] + pltpu.roll(accs[0], 1, 0) * not_first + pltpu.roll(accs[2], MC - 1, 0) * not_last

    def turn(acts, shift, dst):
        def body(j, _):
            a0 = acts[0, pad_at(j, TC, shift), :].astype(F32)
            a1 = acts[1, pad_at(j, TC, shift), :].astype(F32)
            at = rows_at(j, TC)
            dst[pl.ds(0, LANES), at] = a0[:, :LANES].T.astype(BF)
            dst[pl.ds(LANES, LANES), at] = (a0[:, LANES:] + a1[:, :LANES]).T.astype(BF)
            dst[pl.ds(2 * LANES, LANES), at] = a1[:, LANES:].T.astype(BF)
            return 0

        lax.fori_loop(0, px // TC, body, 0)

    load_k1.wait()

    def body(j, _):
        cv[rows_at(j, MC), :] = conv(act1, c, k1, False, j)
        return 0

    lax.fori_loop(0, px // MC, body, 0)
    lane1 = lax.broadcasted_iota(jnp.int32, (1, LANES), 1)
    low1 = lane1 < HEAD_DIM
    load_wi.wait()
    for k in range(3 * heads):
        place = 3 * heads * c + k
        blk = dqkv[pl.ds(0, chans), pl.ds(aligned((place // 2) * LANES, LANES), LANES)].astype(F32)
        blk = jnp.where(place % 2 == 0, blk, pltpu.roll(blk, HEAD_DIM, 1))
        wq[:, pl.ds(k * LANES, LANES)] = jnp.where(low1, blk, 0.0).astype(BF)

    load_ew.wait()
    t = t_act[...]
    t_a = t.astype(BF).astype(F32)
    t_b = (t - t_a).astype(BF).astype(F32)
    row16 = lax.broadcasted_iota(jnp.int32, (16, t.shape[1]), 0)
    t_rows = jnp.where(row16 == 0, t_a, jnp.where(row16 == 1, t_b, jnp.where(row16 == 2, t - t_a - t_b, 0.0)))
    film[...] = total(dot(t_rows.astype(BF), ew[...])) + e_off[...].reshape(1, -1)
    scale2 = 1.0 + film[:, win]
    move2 = film[:, pl.ds(aligned(chans + LANES * c, LANES), WIN)]

    swap_a1.wait()

    def body(j, carry):
        v = cv[rows_at(j, MC), :] + conv(act1, oc, k1, False, j) + offset1
        cv[rows_at(j, MC), :] = v
        return stats_step(v, mask2(j, MC), carry)

    mean2, rstd2 = moments(lax.fori_loop(0, px // MC, body, (zero8, zero8)))
    mul2 = rstd2 * gain2 * scale2
    add2 = (shift2 - mean2 * rstd2 * gain2) * scale2 + move2

    def body(j, _):
        pre = cv[rows_at(j, RC), :] * mul2 + add2
        act2[c, pad_at(j, RC), :] = (pre * sigmoid(pre) * own_f).astype(BF)
        return 0

    lax.fori_loop(0, px // RC, body, 0)
    swap_a2 = swap(act2.at[c, inner], act2.at[c, inner], 3)

    load_k2.wait()

    def body(j, _):
        at = rows_at(j, MC)
        hid[at, :] = conv(act2, c, k2, False, j) + offset2 + xw[at, :].astype(F32)
        return 0

    lax.fori_loop(0, px // MC, body, 0)
    swap_a2.wait()

    def body(j, carry):
        v = hid[rows_at(j, MC), :] + conv(act2, oc, k2, False, j)
        hid[rows_at(j, MC), :] = v
        return stats_step(v, mask2(j, MC), carry)

    mean3, rstd3 = moments(lax.fori_loop(0, px // MC, body, (zero8, zero8)))
    mul3 = rstd3 * gain3
    add3 = shift3 - mean3 * mul3

    def body(j, _):
        act3[c, rows_at(j, RC), :] = ((hid[rows_at(j, RC), :] * mul3 + add3) * own_f).astype(BF)
        return 0

    lax.fori_loop(0, px // RC, body, 0)
    swap_a3 = swap(act3.at[c], act3.at[c], 4)

    biases = []
    for h in range(heads):
        blk = off_in[pl.ds(aligned(LANES * (heads * c + h), LANES), LANES)].reshape(1, LANES)
        turned = pltpu.roll(jnp.broadcast_to(blk, (8, LANES)), HEAD_DIM, 1)[:1]
        bias_q = jnp.where(low1, blk, jnp.where(lane1 == HEAD_DIM, 8.0, 0.0))
        bias_v = jnp.where(low1, turned, jnp.where(lane1 < HEAD_DIM + 2, 1.0, 0.0))
        biases.append((bias_q, bias_v))
    load_wo.wait()
    load_g.wait()
    swap_g.wait()
    wo_rows = pl.ds(aligned(own_chans * c, HEAD_DIM), own_chans)

    def body(j, _):
        o = dot_nt(wo[wo_rows, :], gf[rows_at(j, MC), :])
        for h in range(heads):
            dot_t[h, pl.ds(0, HEAD_DIM), rows_at(j, MC)] = o[HEAD_DIM * h : HEAD_DIM * (h + 1)].astype(BF)
        return 0

    lax.fori_loop(0, px // MC, body, 0)

    turn(act1, side, act_t1)
    turn(act2, side, act_t2)
    swap_a3.wait()

    def body(j, _):
        at = rows_at(j, MC)
        a0 = act3[0, at, :]
        a1 = act3[1, at, :]
        hidden_key = (mask[at, :] == 0.0) & (lane1 == HEAD_DIM)
        for h in range(heads):
            cols = pl.ds(3 * LANES * h, 3 * LANES)
            o = dot(a0, wq[pl.ds(0, WIN), cols]) + dot(a1, wq[pl.ds(LANES, WIN), cols])
            q = (o[:, :LANES] + biases[h][0]).astype(BF).astype(F32) * 0.125
            k = jnp.where(hidden_key, MASKED, o[:, LANES : 2 * LANES])
            v = o[:, 2 * LANES :] + biases[h][1]
            qa[h, at, :] = q.astype(BF)
            ka[h, at, :] = k.astype(BF)
            va[h, at, :] = v.astype(BF)
            kat[h, :, at] = k.T.astype(BF)
            vat[h, :, at] = v.T.astype(BF)
        return 0

    lax.fori_loop(0, px // MC, body, 0)

    row128 = lax.broadcasted_iota(jnp.int32, (LANES, px), 0)

    def body(h, _):
        qc = qa[h]
        scores = dot_nt(ka[h], qc)
        top = jnp.max(scores, axis=0, keepdims=True)
        e = jnp.exp(scores - top).astype(BF)
        o = dot(vat[h], e)
        inv = 1.0 / o[HEAD_DIM : HEAD_DIM + 1, :]
        o = o * inv
        att_t[pl.ds(aligned(HEAD_DIM * h, HEAD_DIM), HEAD_DIM), :] = o[:HEAD_DIM].astype(BF)
        g = dot_t[h].astype(F32)
        less = -inv * jnp.sum(g * o, axis=0, keepdims=True)
        high = less.astype(BF).astype(F32)
        g = jnp.where(row128 == HEAD_DIM, high, jnp.where(row128 == HEAD_DIM + 1, less - high, g * inv)).astype(BF)
        ds = (e.astype(F32) * dot(va[h], g)).astype(BF)
        grads = (dot(kat[h], ds).T * 0.125, dot(ds, qc), dot_nt(e, g))
        for k, d in enumerate(grads):
            dqkv[:, pl.ds(aligned((3 * h + k) * LANES, LANES), LANES)] = jnp.where(low1, d, 0.0).astype(BF)
        return 0

    lax.fori_loop(0, heads, body, 0, unroll=True)

    def body(j, _):
        at = rows_at(j, MC)
        datt_s[at, :] = dot_nt(dqkv[at, :], wq[owin, :]).astype(BF)
        return 0

    lax.fori_loop(0, px // MC, body, 0)
    swap_da = swap(datt_s, datt_r, 5)

    def body(j, _):
        at = rows_at(j, MC)
        tmp[at, :] = dot_nt(dqkv[at, :], wq[win, :])
        return 0

    lax.fori_loop(0, px // MC, body, 0)
    turn(act3, 0, act_t3)

    used = [0]
    flows = {}

    def flow_of(key, pay, rbuf, gathered, order, base, size):
        if size:
            flow = Flow(pay, rbuf, gathered, base, size, stages(order), (fs, fr, used[0]), c, img)
            used[0] += flow_sems
            flows[key] = flow
            flow.advance()

    def advance(point):
        for key in PLAN[point]:
            if key in flows:
                flows[key].advance()

    def hand_out(key):
        flow = flows.pop(key)
        for cp in flow.forwards:
            cp.wait()

    swap_da.wait()

    def back_sums(carry, u, normed):
        return carry[0] + fold(u), carry[1] + fold(u * normed)

    def body(j, carry):
        at = rows_at(j, RC)
        u = tmp[at, :] + datt_r[at, :].astype(F32)
        tmp[at, :] = u
        return back_sums(carry, u, (hid[at, :] - mean3) * rstd3)

    s0, s1 = lax.fori_loop(0, px // RC, body, (zero8, zero8))
    vx[pl.ds(6, 1), win] = total(s1) * own_f
    vx[pl.ds(7, 1), win] = total(s0) * own_f

    def spread_of(s0, s1, gain):
        a, b = group_totals(s0 * gain, s1 * gain)
        return a * inv_entries, b * inv_entries

    sp_a, sp_b = spread_of(s0, s1, gain3)

    def body(j, carry):
        at = rows_at(j, RC)
        normed = (hid[at, :] - mean3) * rstd3
        d = gf[at, win].astype(F32) + rstd3 * (tmp[at, :] * gain3 - mask2(j) * (sp_a + normed * sp_b))
        resid[at, :] = d
        low = (d * own_f).astype(BF)
        dd2[c, pad_at(j, RC), :] = low
        return carry + fold(low.astype(F32))

    vx[pl.ds(5, 1), win] = total(lax.fori_loop(0, px // RC, body, zero8))
    swap_d2 = swap(dd2.at[c, inner], dd2.at[c, inner], 7)

    own_lanes = pl.ds(aligned(LANES * c, LANES), LANES)
    mid_lanes = pl.ds(aligned(LANES * oc, LANES), LANES)
    hc = chans // 2
    my_half = pl.ds(aligned(hc * c, HEAD_DIM), hc)

    def shift_into(first_lane, read):
        lanes = pl.ds(first_lane, LANES)

        def body(j, _):
            at = pad_at(j, TC)
            d = read(at)
            dm[0, at, lanes] = (pltpu.roll(d, TC - 1, 0) * not_last[:TC, :LANES]).astype(BF)
            dm[1, at, lanes] = d.astype(BF)
            dm[2, at, lanes] = (pltpu.roll(d, 1, 0) * not_first[:TC, :LANES]).astype(BF)
            return 0

        lax.fori_loop(0, px // TC, body, 0)

    def kernel_grad(act_t, dd, wait, key, pay, rbuf, gathered, point):
        unit = 16 * n_img
        sizes = [units * unit for units in shares(pay.shape[0] // unit, KERNEL_FLOWS)]
        begun = []

        def begin(rows):
            while len(begun) < len(sizes) and sum(sizes[: len(begun) + 1]) <= rows:
                k = len(begun)
                flow_of(key + k, pay, rbuf, gathered, KERNEL_FLOWS[k][0], sum(sizes[:k]), sizes[k])
                begun.append(k)

        def tap_rows(tap, lanes):
            return dm[tap % 3, pl.ds(side * (2 - tap // 3), px), lanes]

        def block(rows, base, lanes):
            n = rows.shape[0]
            for tap in range(0, 9, 2):
                if tap < 8:
                    o = dot(rows[...], jnp.concatenate([tap_rows(tap, lanes), tap_rows(tap + 1, lanes)], axis=1))
                    pay[pl.ds(base + tap * n, n), :] = o[:, :LANES].astype(BF)
                    pay[pl.ds(base + (tap + 1) * n, n), :] = o[:, LANES:].astype(BF)
                else:
                    pay[pl.ds(base + tap * n, n), :] = dot(rows[...], tap_rows(tap, lanes)).astype(BF)
                begin(base + min(tap + 2, 9) * n)

        shift_into(0, lambda at: dd[c, at, own_lanes].astype(F32))
        block(act_t, 0, pl.ds(0, LANES))
        if point is not None:
            advance(point)
        wait()
        shift_into(LANES, lambda at: dd[c, at, mid_lanes].astype(F32) + dd[oc, at, own_lanes].astype(F32))
        block(act_t.at[my_half], 9 * chans, pl.ds(LANES, LANES))
        begin(pay.shape[0])

    kernel_grad(act_t2, dd2, swap_d2.wait, SECOND[0], pay2, rb2, out2, None)

    def body(j, carry):
        at = rows_at(j, MC)
        pre = cv[at, :] * mul2 + add2
        sg = sigmoid(pre)
        u = (conv(dd2, c, k2, True, j) + conv(dd2, oc, k2, True, j)) * (sg * (1.0 + pre * (1.0 - sg)))
        tmp[at, :] = u
        return back_sums(carry, u, (cv[at, :] - mean2) * rstd2)

    s0, s1 = lax.fori_loop(0, px // MC, body, (zero8, zero8))
    advance(0)
    t0, t1 = total(s0), total(s1)
    vx[pl.ds(9, 1), win] = (gain2 * t1 + shift2 * t0) * own_f
    vx[pl.ds(10, 1), win] = t0 * own_f
    vx[pl.ds(3, 1), win] = scale2 * t1 * own_f
    vx[pl.ds(4, 1), win] = scale2 * t0 * own_f
    gain2s = gain2 * scale2
    sp_a, sp_b = spread_of(s0, s1, gain2s)

    def body(j, carry):
        at = rows_at(j, RC)
        normed = (cv[at, :] - mean2) * rstd2
        d = rstd2 * (tmp[at, :] * gain2s - mask2(j) * (sp_a + normed * sp_b))
        low = (d * own_f).astype(BF)
        dd1[c, pad_at(j, RC), :] = low
        return carry + fold(low.astype(F32))

    vx[pl.ds(2, 1), win] = total(lax.fori_loop(0, px // RC, body, zero8))
    swap_d1 = swap(dd1.at[c, inner], dd1.at[c, inner], 8)

    advance(1)

    kernel_grad(act_t1, dd1, swap_d1.wait, FIRST[0], pay1, rb1, out1, 2)
    advance(3)

    for k in range(3 * heads // 2):
        o = dot(act_t3[...], dqkv[:, pl.ds(2 * LANES * k, 2 * LANES)])
        pair = o[:, :LANES] + pltpu.roll(o[:, LANES:], HEAD_DIM, 1)
        payp[pl.ds(k * chans, chans), :] = pair.astype(BF)
    base = (3 * heads // 2) * chans
    if (3 * heads) % 2:
        o = dot(act_t3[...], dqkv[:, pl.ds((3 * heads - 1) * LANES, LANES)])
        pair = o[: chans // 2] + pltpu.roll(o[chans // 2 :], HEAD_DIM, 1)
        payp[pl.ds(base, chans // 2), :] = pair.astype(BF)
        base += chans // 2
    o = dot(att_t[pl.ds(0, own_chans), :], gf[...])
    for b in range(chans // LANES):
        payp[pl.ds(base + b * own_chans, own_chans), :] = o[:, b * LANES : (b + 1) * LANES].astype(BF)

    for h in range(heads):
        z = jnp.zeros((8, LANES), F32)

        def body(j, carry, h=h):
            at = rows_at(j, TC)
            q = dqkv[at, pl.ds(3 * h * LANES, LANES)].astype(F32)
            v = dqkv[at, pl.ds((3 * h + 2) * LANES, LANES)].astype(F32)
            return carry[0] + fold(q), carry[1] + fold(v)

        sum_q, sum_v = lax.fori_loop(0, px // TC, body, (z, z))
        sums = total(sum_q + pltpu.roll(sum_v, HEAD_DIM, 1))
        vx[pl.ds(13, 1), pl.ds(LANES * h, LANES)] = jnp.where(first, sums, 0.0)
        vx[pl.ds(14, 1), pl.ds(LANES * h, LANES)] = jnp.where(first, 0.0, sums)

    advance(4)
    at = 0
    for k, units in enumerate(shares(payp.shape[0] // (16 * n_img), PROJECT_FLOWS)):
        flow_of(PROJECT[0] + k, payp, rbp, outp, PROJECT_FLOWS[k][0], at, units * 16 * n_img)
        at += units * 16 * n_img

    def body(j, carry):
        at = rows_at(j, MC)
        x = xw[at, :].astype(F32)
        pre = x * mul1 + add1
        sg = sigmoid(pre)
        u = (conv(dd1, c, k1, True, j) + conv(dd1, oc, k1, True, j)) * (sg * (1.0 + pre * (1.0 - sg)))
        tmp[at, :] = u
        return back_sums(carry, u, (x - mean1) * rstd1)

    s0, s1 = lax.fori_loop(0, px // MC, body, (zero8, zero8))
    advance(5)
    vx[pl.ds(0, 1), win] = total(s1) * own_f
    vx[pl.ds(1, 1), win] = total(s0) * own_f

    g_sum = jnp.zeros((8, chans), F32)

    def body(j, carry):
        return carry + fold(gf[rows_at(j, RC), :].astype(F32))

    g_sum = total(lax.fori_loop(0, px // RC, body, g_sum))
    vx[pl.ds(8, 1), :] = jnp.where(first, g_sum, 0.0)
    for k in range(2):
        vx[pl.ds(11 + k, 1), :] = jnp.where(first, t_act[:, pl.ds(k * chans, chans)], 0.0)
    swap_v = swap(vx, vr, 9)

    sp_a, sp_b = spread_of(s0, s1, gain1)

    def body(j, _):
        at = rows_at(j, RC)
        normed = (xw[at, :].astype(F32) - mean1) * rstd1
        d = resid[at, :] + rstd1 * (tmp[at, :] * gain1 - mask2(j) * (sp_a + normed * sp_b))
        tmp[at, :] = d * own_f
        datt_s[at, :] = (d * own_f).astype(BF)
        return 0

    lax.fori_loop(0, px // RC, body, 0)
    swap_i = swap(datt_s.at[other_rows], ing_r, 10)

    swap_v.wait()
    vall[img] = vx[...] + vr[...]

    class Gather:
        def __init__(self):
            self.k = -1
            self.copies = []

        def advance(self):
            for cp in self.copies:
                cp.wait()
            self.copies = []
            self.k += 1
            if self.k < nbits:
                bit = bits[self.k]
                at = vall.at[pl.ds((img // bit) * bit, bit)]
                k = used[0]
                used[0] += 1
                cp = pltpu.make_async_remote_copy(
                    src_ref=at, dst_ref=at, send_sem=fs.at[k], recv_sem=fr.at[k],
                    device_id=(xor(img, [bit], 1), c), device_id_type=MESH,
                )
                cp.start()
                self.copies.append(cp)

    vectors = Gather()
    vectors.advance()
    advance(6)

    def body(j, _):
        at = rows_at(j, TC)
        tsum[at, :] = dot(att_t[:, at].astype(F32).T.astype(BF), wo[pl.ds(aligned(own_chans * c, HEAD_DIM), WIN), :])
        tsum[at, win] += hid[at, :] * own_f
        return 0

    lax.fori_loop(0, px // TC, body, 0)
    swap_t = swap(tsum.at[other_rows], trecv, 6)

    advance(7)
    vectors.advance()

    swap_t.wait()
    res_v[...] = (tsum[my_rows, :] + trecv[...] + p_oo[...].reshape(1, -1)).astype(BF)
    swap_i.wait()
    top_rows = pl.ds(0, half)
    tsum[top_rows, :] = jnp.zeros((half, chans), F32)
    tsum[top_rows, win] = tmp[my_rows, :]
    tsum[top_rows, owin] += ing_r[...].astype(F32)
    ing_v[...] = tsum[top_rows, :].astype(BF)
    ended = {}
    for n, key in enumerate(PLAN[8]):
        if key in flows:
            flows[key].advance()
            if flows[key].ended():
                ended.setdefault(key, n)
        if n % 8 == 7:
            vectors.advance()
        for key in [k for k in ended if ended[k] + 6 == n]:
            hand_out(key)
    while any(not flow.ended() for flow in flows.values()):
        for flow in flows.values():
            flow.advance()
        vectors.advance()
    while vectors.copies:
        vectors.advance()
    for key in sorted(flows, key=lambda k: ended.get(k, 0)):
        hand_out(key)


def finish_kernel(dims, b1, b2, bp, bv, res, ing, *refs):
    chans, heads = dims
    (res_o, ing_o, g1, s1, k1o, o1, ewo, eoo, g2, s2, k2o, o2, g3, s3, pio, oio, poo, ooo) = refs[:18]
    (f1, f2, fe, fi, fo, fw, fv, osem) = refs[18:]
    hc = chans // 2
    own = chans // 2
    te = fe.shape[0]

    def move(src, dst, sem):
        cp = pltpu.make_async_copy(src, dst, sem)
        cp.start()
        return cp

    out = [move(res, res_o, osem.at[0]), move(ing, ing_o, osem.at[1])]

    def kernel(n, pay, full, dst):
        for a in range(3):

            def body(b, _, a=a):
                tap = 3 * a + b
                at = main = pl.ds(pl.multiple_of(tap * chans, LANES), chans)
                full[at, pl.ds(0, LANES)] = pay[0, main, :].astype(F32)
                full[at, pl.ds(2 * LANES, LANES)] = pay[1, main, :].astype(F32)
                mid = pl.ds(pl.multiple_of(9 * chans + tap * hc, HEAD_DIM), hc)
                for s in range(2):
                    to = pl.ds(pl.multiple_of(tap * chans + s * hc, HEAD_DIM), hc)
                    full[to, pl.ds(LANES, LANES)] = pay[s, mid, :].astype(F32)
                return 0

            lax.fori_loop(0, 3, body, 0)
            part = pl.ds(3 * a * chans, 3 * chans)
            out.append(move(full.at[part], dst.at[part], osem.at[3 + 3 * n + a]))

    kernel(0, b2, f2, k2o)

    sums = jnp.sum(bv[...], axis=0)
    for n, (dst, k) in enumerate(((g1, 0), (s1, 1), (o1, 2), (g2, 3), (s2, 4), (o2, 5), (g3, 6), (s3, 7), (ooo, 8))):
        at = pl.ds(n * chans, chans)
        fv[at] = sums[k]
        out.append(move(fv.at[at], dst, osem.at[11 + n]))
    for n, (dst, k) in enumerate(((eoo, 9), (oio, 13))):
        at = pl.ds(2 * n * chans, 2 * chans)
        fw[pl.ds(2 * n * chans, chans)] = sums[k]
        fw[pl.ds((2 * n + 1) * chans, chans)] = sums[k + 1]
        out.append(move(fw.at[at], dst, osem.at[20 + n]))
    for a in range(2):
        for b in range(2):
            fe[pl.ds(a * chans, chans), pl.ds(b * chans, chans)] = lax.dot_general(
                bv[:, 11 + a, :], bv[:, 9 + b, :], (((0,), (0,)), ((), ())),
                preferred_element_type=F32, precision=lax.Precision.HIGHEST,
            )
    out.append(move(fe, ewo, osem.at[2]))

    kernel(1, b1, f1, k1o)

    low = lax.broadcasted_iota(jnp.int32, (1, LANES), 1) < HEAD_DIM
    pairs = 3 * heads // 2
    odd = (3 * heads) % 2
    sides = []
    for s in range(2):
        blocks = [bp[s, pl.ds(k * chans, chans), :].astype(F32) for k in range(pairs)]
        if odd:
            last = bp[s, pl.ds(pairs * chans, chans // 2), :].astype(F32)
            blocks.append(jnp.concatenate([last, pltpu.roll(last, HEAD_DIM, 1)], axis=0))
        sides.append(blocks)
    cols = sides[0] + sides[1]
    if odd:
        turned = [pltpu.roll(b, HEAD_DIM, 1) for b in sides[1]]
        cols = sides[0][:-1] + [jnp.where(low, sides[0][-1], turned[0])]
        cols += [jnp.where(low, turned[k], turned[k + 1]) for k in range(pairs)]
    for k, b in enumerate(cols):
        fi[:, pl.ds(k * LANES, LANES)] = b
    out.append(move(fi, pio, osem.at[9]))
    base = pairs * chans + odd * (chans // 2)
    for s in range(2):
        for b in range(chans // LANES):
            fo[pl.ds(s * own, own), pl.ds(b * LANES, LANES)] = bp[s, pl.ds(base + b * own, own), :].astype(F32)
    out.append(move(fo, poo, osem.at[10]))
    for cp in out:
        cp.wait()


def time_features(timesteps, width):
    half_width = width // 2
    frequency = jnp.exp(-math.log(10000.0) * jnp.arange(half_width, dtype=jnp.float32) / half_width)
    angles = timesteps.astype(jnp.float32)[:, None] * frequency[None, :]
    return jnp.concatenate([jnp.cos(angles), jnp.sin(angles)], axis=1)


def local(
    n_img,
    images_in, extents, timesteps, gain_first, shift_first, kernel_first, offset_first, embed_weight, embed_offset,
    gain_second, shift_second, kernel_second, offset_second, gain_attend, shift_attend, project_in, offset_in,
    project_out, offset_out, out_grad,
):
    _, stripe_rows, side, chans = images_in.shape
    px = side * side
    half = stripe_rows * side
    te = embed_weight.shape[0]
    own = chans // 2
    heads = own // HEAD_DIM
    taps = 9
    unit = 16 * n_img
    real_k = taps * (chans + chans // 2)
    real_p = 3 * heads * HEAD_DIM * chans // LANES + own * (chans // LANES)
    rows_k = cdiv(real_k, unit) * unit
    rows_p = cdiv(real_p, unit) * unit
    bits = []
    while 2 ** len(bits) < n_img:
        bits.append(2 ** len(bits))
    nbits = len(bits)

    t_act = jax.nn.silu(time_features(timesteps, te))
    vm = pl.BlockSpec(memory_space=pltpu.VMEM)
    anym = pl.BlockSpec(memory_space=pl.ANY)
    smem = pl.BlockSpec(memory_space=pltpu.SMEM)
    sds = jax.ShapeDtypeStruct
    V = pltpu.VMEM
    padded = px + 2 * side
    wide = 3 * heads * LANES
    flow_sems = 2 * nbits + 2
    n_sem = (2 * len(KERNEL_FLOWS) + len(PROJECT_FLOWS)) * flow_sems + nbits
    scratch = [
        V((taps * chans, chans), BF), V((taps * chans, chans), BF),
        V((chans + WIN - own, chans), BF), V((te, 2 * chans), BF), V((chans, wide), BF),
        V((px, WIN), BF), V((px, chans), BF), V((px, LANES), F32), V((1, 2 * chans), F32),
        V((2, padded, WIN), BF), V((2, padded, WIN), BF), V((2, px, WIN), BF), V((2, padded, WIN), BF), V((2, padded, WIN), BF),
        V((px, WIN), F32), V((px, WIN), F32), V((px, WIN), F32), V((px, WIN), F32),
        V((heads, px, LANES), BF), V((heads, px, LANES), BF), V((heads, px, LANES), BF),
        V((heads, LANES, px), BF), V((heads, LANES, px), BF), V((heads, LANES, px), BF), V((WIN, px), BF), V((px, wide), BF),
        V((px, chans), F32), V((half, chans), F32), V((px, WIN), BF), V((px, WIN), BF),
        V((3, padded, WIN), BF), V((chans, px), BF), V((chans, px), BF), V((chans, px), BF), V((half, WIN), BF),
        V((rows_k, LANES), BF), V((rows_k, LANES), BF), V((rows_p, LANES), BF),
        V((rows_k, LANES), BF), V((rows_k, LANES), BF), V((rows_p, LANES), BF),
        V((16, chans), F32), V((16, chans), F32),
        pltpu.SemaphoreType.DMA((7,)), pltpu.SemaphoreType.DMA((11,)), pltpu.SemaphoreType.DMA((11,)),
        pltpu.SemaphoreType.DMA((n_sem,)), pltpu.SemaphoreType.DMA((n_sem,)),
    ]
    res, ing, pk1, pk2, pp, vec = pl.pallas_call(
        functools.partial(block_kernel, (side, chans, n_img, real_k, real_p, tuple(bits), flow_sems)),
        out_shape=(
            V((half, chans), BF), V((half, chans), BF), V((2, rows_k, LANES), BF), V((2, rows_k, LANES), BF),
            V((2, rows_p, LANES), BF), V((n_img, 16, chans), F32),
        ),
        in_specs=[anym, anym, smem] + [vm] * 12 + [anym, anym, anym, anym, anym],
        out_specs=(vm,) * 6,
        scratch_shapes=scratch,
        compiler_params=pltpu.CompilerParams(collective_id=0, has_side_effects=True, vmem_limit_bytes=50 * 2**20),
        cost_estimate=pl.CostEstimate(flops=2 * 10**10, bytes_accessed=2 * 10**7, transcendentals=4 * 10**6),
        name="block",
    )(
        images_in.reshape(half, chans), out_grad.reshape(half, chans), extents, gain_first, shift_first, offset_first,
        gain_second, shift_second, offset_second, gain_attend, shift_attend, offset_out, t_act, embed_offset, offset_in,
        kernel_first.reshape(taps * chans, chans), kernel_second.reshape(taps * chans, chans),
        project_in, project_out, embed_weight,
    )

    row = sds((chans,), F32)
    row2 = sds((2 * chans,), F32)
    kern = sds((taps * chans, chans), F32)
    stripe = sds((half, chans), BF)
    outs = pl.pallas_call(
        functools.partial(finish_kernel, (chans, heads)),
        out_shape=(
            stripe, stripe, row, row, kern, row, sds((te, 2 * chans), F32), row2, row, row, kern, row, row, row,
            sds((chans, 3 * chans), F32), row2, sds((chans, chans), F32), row,
        ),
        in_specs=[vm] * 6,
        out_specs=(anym,) * 18,
        scratch_shapes=[
            V((taps * chans, chans), F32), V((taps * chans, chans), F32), V((te, 2 * chans), F32),
            V((chans, 3 * chans), F32), V((chans, chans), F32), V((4 * chans,), F32), V((9 * chans,), F32),
            pltpu.SemaphoreType.DMA((22,)),
        ],
        compiler_params=pltpu.CompilerParams(vmem_limit_bytes=32 * 2**20),
        cost_estimate=pl.CostEstimate(flops=10**8, bytes_accessed=23 * 10**6, transcendentals=0),
        name="finish",
    )(*(pltpu.with_memory_space_constraint(x, pltpu.VMEM) for x in (pk1, pk2, pp, vec, res, ing)))
    res, ing, *outs = outs
    shapes = (
        gain_first, shift_first, kernel_first, offset_first, embed_weight, embed_offset, gain_second, shift_second,
        kernel_second, offset_second, gain_attend, shift_attend, project_in, offset_in, project_out, offset_out,
    )
    outs = [o.reshape(s.shape) for o, s in zip(outs, shapes)]
    return (res.reshape(images_in.shape), ing.reshape(images_in.shape), *outs)


def solution(mesh):
    n_img = mesh.shape["img"]
    stripe = P("img", "pix", None, None)
    in_specs = (stripe, P("img", None), P("img")) + (P(),) * 16 + (stripe,)
    out_specs = (stripe, stripe) + (P(),) * 16
    return jax.shard_map(
        functools.partial(local, n_img), mesh=mesh, in_specs=in_specs, out_specs=out_specs, check_vma=False
    )
```

```python
import functools
import math

import jax
import jax.numpy as jnp
from jax import lax
from jax.experimental import pallas as pl
from jax.experimental.pallas import tpu as pltpu
from jax.sharding import PartitionSpec as P

HEAD_DIM = 64
GROUPS = 32
EPSILON = 1e-05
MASKED = -1e30
BF = jnp.bfloat16
F32 = jnp.float32
MESH = pl.DeviceIdType.MESH
WIN = 256
LANES = 128
RC = 256
MC = 512
TC = 256
X_FIRST, Y_FIRST, Z_FIRST = (0, 1, 2, 3), (1, 2, 0, 3), (2, 0, 1, 3)
KERNEL_FLOWS = ((Z_FIRST, 4), (X_FIRST, 4), (Y_FIRST, 4), (Z_FIRST, 3), (X_FIRST, 3), (Y_FIRST, 3))
PROJECT_FLOWS = ((X_FIRST, 3), (Y_FIRST, 3), (Z_FIRST, 3))
SECOND, FIRST, PROJECT = tuple(range(16)), tuple(range(16, 32)), tuple(range(32, 48))
PLAN = (
    (),
    SECOND,
    (),
    (),
    SECOND,
    SECOND + FIRST + PROJECT,
    (),
    SECOND + FIRST + PROJECT,
    (),
)


def dot(a, b):
    return jnp.dot(a, b, preferred_element_type=F32)


def dot_nt(a, b):
    return lax.dot_general(a, b, (((1,), (1,)), ((), ())), preferred_element_type=F32)


def dot_hi(a, b):
    return jnp.dot(a, b, preferred_element_type=F32, precision=lax.Precision.HIGHEST)


def fold(v):
    return jnp.sum(v.reshape(v.shape[0] // 8, 8, v.shape[1]), axis=0)


def sigmoid(v):
    return 1.0 / (1.0 + jnp.exp(-v))


def cdiv(a, b):
    return -(-a // b)


def xor(img, bits, d):
    for pos, bit in enumerate(bits):
        if (d >> pos) & 1:
            img = img + bit * (1 - 2 * ((img // bit) % 2))
    return img


def index_in(img, bits, d=0):
    v = 0
    for pos, bit in enumerate(bits):
        mine = (img // bit) % 2
        v = v + ((1 - mine) if (d >> pos) & 1 else mine) * (1 << pos)
    return v


def shares(total, flows):
    weight = sum(w for _, w in flows)
    ends = [0]
    for k in range(len(flows)):
        ends.append(-(-total * sum(w for _, w in flows[: k + 1]) // weight))
    return [b - a for a, b in zip(ends, ends[1:])]


class Flow:
    def __init__(self, pay, rbuf, out, base, rows, stages, sems, core, img):
        self.pay, self.rbuf, self.out, self.lo, self.size = pay, rbuf, out, base, rows
        self.base, self.rows = base, rows
        self.rbase, self.stages, self.sems, self.core, self.img = base, stages, sems, core, img
        self.k = -1
        self.used = 0
        self.copies = []
        self.forwards = []

    def send(self, src, dst, device):
        send, recv, first = self.sems
        cp = pltpu.make_async_remote_copy(
            src_ref=src, dst_ref=dst, send_sem=send.at[first + self.used], recv_sem=recv.at[first + self.used],
            device_id=device, device_id_type=MESH,
        )
        self.used += 1
        cp.start()
        return cp

    def forward(self, lo, size):
        ref = self.out.at[self.core, pl.ds(pl.multiple_of(lo, 16), size)]
        self.forwards.append(self.send(ref, ref, (self.img, 1 - self.core)))

    def start(self):
        n = len(self.stages)
        self.copies = []
        if self.k < n:
            bits = self.stages[self.k]
            part = self.size >> len(bits)
            for d in range(1, 1 << len(bits)):
                lo = pl.multiple_of(self.lo + index_in(self.img, bits, d) * part, 16)
                src = self.pay.at[pl.ds(lo, part)]
                dst = self.rbuf.at[pl.ds(self.rbase + (d - 1) * part, part)]
                self.copies.append(self.send(src, dst, (xor(self.img, bits, d), self.core)))
        else:
            bits = self.stages[2 * n - 1 - self.k]
            ref = self.out.at[self.core, pl.ds(self.lo, self.size)]
            for d in range(1, 1 << len(bits)):
                self.copies.append(self.send(ref, ref, (xor(self.img, bits, d), self.core)))
            if self.k == 2 * n - 1:
                self.forward(self.lo, self.size)

    def finish(self):
        n = len(self.stages)
        for cp in self.copies:
            cp.wait()
        if self.k < n:
            bits = self.stages[self.k]
            more = (1 << len(bits)) - 1
            part = self.size >> len(bits)
            keep = pl.multiple_of(self.lo + index_in(self.img, bits) * part, 16)
            rbase = self.rbase
            step = 16
            for cand in (512, 448, 256, 128, 112, 64, 48, 32):
                if part % cand == 0:
                    step = cand
                    break

            def add(j, _):
                at = pl.ds(pl.multiple_of(keep + j * step, 16), step)
                v = self.pay[at, :].astype(F32)
                for d in range(more):
                    v = v + self.rbuf[pl.ds(pl.multiple_of(rbase + d * part + j * step, 16), step), :].astype(F32)
                if self.k == n - 1:
                    self.out[self.core, at, :] = v.astype(BF)
                else:
                    self.pay[at, :] = v.astype(BF)
                return 0

            lax.fori_loop(0, part // step, add, 0)
            self.lo, self.size = keep, part
            self.rbase += more * part
        else:
            bits = self.stages[2 * n - 1 - self.k]
            mine = index_in(self.img, bits)
            whole = pl.multiple_of(self.lo - mine * self.size, 16)
            if self.k == 2 * n - 1:
                for d in range(1, 1 << len(bits)):
                    self.forward(whole + index_in(self.img, bits, d) * self.size, self.size)
            self.lo = whole
            self.size <<= len(bits)

    def ended(self):
        return self.k >= 2 * len(self.stages)

    def advance(self):
        last = 2 * len(self.stages)
        if self.ended():
            return
        if self.k >= 0:
            self.finish()
        self.k += 1
        if self.k < last:
            self.start()


def block_kernel(dims, *refs):
    side, chans, n_img, real_k, real_p, bits, flow_sems = dims
    (
        x_in, g_in, ext, h_g1, h_s1, h_o1, h_g2, h_s2, h_o2, h_g3, h_s3, h_oo, h_t, h_eo, h_oi, k1_h, k2_h, wi_h, wo_h, ew_h,
        res_v, ing_v, out1, out2, outp, vall,
        k1, k2, wo, ew, wq, xw, gf, mask, film, act1, act2, act3, dd2, dd1,
        cv, hid, tmp, resid, qa, ka, va, kat, vat, dot_t, att_t, dqkv,
        tsum, trecv, datt_s, datt_r, dm, act_t1, act_t2, act_t3, ing_r,
        pay1, pay2, payp, rb1, rb2, rbp, vx, vr,
        p_g1, p_s1, p_o1, p_g2, p_s2, p_o2, p_g3, p_s3, p_oo, t_act, e_off, off_in,
        lsem, xs, xr, fs, fr,
    ) = refs
    img = lax.axis_index("img")
    c = lax.axis_index("pix")
    oc = 1 - c
    px = side * side
    half = px // 2
    own_chans = chans // 2
    heads = own_chans // HEAD_DIM
    first = c == 0
    nbits = len(bits)

    def aligned(v, m):
        return pl.multiple_of(v, m)

    def rows_at(j, size):
        return pl.ds(aligned(j * size, size), size)

    def pad_at(j, size, shift=side):
        return pl.ds(aligned(j * size + shift, 32), size)

    win = pl.ds(aligned(LANES * c, LANES), WIN)
    owin = pl.ds(aligned(LANES * oc, LANES), WIN)

    barrier = pltpu.get_barrier_semaphore()
    peers = [(img, oc)]

    def stages(order):
        near = [bits[k] for k in order if k < nbits]
        return [[bit] for bit in near + list(bits[len(order) :])]

    for bit in bits:
        peers.append((xor(img, [bit], 1), c))
    for peer in peers:
        pl.semaphore_signal(barrier, inc=1, device_id=peer, device_id_type=MESH)

    loads = []
    my_rows = pl.ds(aligned(half * c, half), half)
    other_rows = pl.ds(aligned(half * oc, half), half)
    copies = (
        (x_in.at[:, win], xw.at[my_rows]),
        (wi_h, dqkv.at[pl.ds(0, chans)]),
        (h_g1, p_g1),
        (h_s1, p_s1),
        (h_o1, p_o1),
        (h_g2, p_g2),
        (h_s2, p_s2),
        (h_o2, p_o2),
        (h_g3, p_g3),
        (h_s3, p_s3),
        (h_oo, p_oo),
        (h_t, t_act),
        (h_eo, e_off),
        (h_oi, off_in),
        (ew_h, ew),
        (k1_h, k1),
        (g_in, gf.at[my_rows]),
        (wo_h, wo.at[pl.ds(0, chans)]),
        (k2_h, k2),
    )
    for k, (src, dst) in enumerate(copies):
        cp = pltpu.make_async_copy(src, dst, lsem.at[k])
        cp.start()
        loads.append(cp)
    load_x, load_wi, *small, load_ew, load_k1, load_g, load_wo, load_k2 = loads

    lane = lax.broadcasted_iota(jnp.int32, (1, WIN), 1)
    own_f = (jnp.where(first, lane, WIN - 1 - lane) < own_chans).astype(F32)
    rows_e = ext[0, 0]
    cols_e = ext[0, 1]
    per = chans // GROUPS
    inv_entries = 1.0 / jnp.full((1, WIN), rows_e * cols_e * per, jnp.int32).astype(F32)
    gi = lax.broadcasted_iota(jnp.int32, (WIN, WIN), 0) + LANES * c
    gj = lax.broadcasted_iota(jnp.int32, (WIN, WIN), 1) + LANES * c
    same = (gi // per == gj // per).astype(F32).astype(BF)

    def group_totals(a, b):
        both = jnp.concatenate([a, b], axis=0)
        high = both.astype(BF)
        rest = both - high.astype(F32)
        mid = rest.astype(BF)
        low = (rest - mid.astype(F32)).astype(BF)
        o = dot(jnp.concatenate([high, mid, low], axis=0), same)
        o = o[:16] + o[16:32] + o[32:]
        return jnp.sum(o[:8], axis=0, keepdims=True), jnp.sum(o[8:], axis=0, keepdims=True)

    def total(a):
        return jnp.sum(a, axis=0, keepdims=True)

    zero8 = jnp.zeros((8, WIN), F32)

    def fill_mask(j, _):
        p = lax.broadcasted_iota(jnp.int32, (RC, LANES), 0) + j * RC
        ok = (p // side < rows_e) & (p % side < cols_e)
        mask[rows_at(j, RC), :] = ok.astype(F32)
        return 0

    lax.fori_loop(0, px // RC, fill_mask, 0)

    def mask2(j, size=RC):
        m = mask[rows_at(j, size), :]
        return jnp.concatenate([m, m], axis=1)

    edge = jnp.zeros((side, WIN), BF)
    for buf in (act1, act2, dd2, dd1):
        for s in range(2):
            buf[s, pl.ds(0, side), :] = edge
            buf[s, pl.ds(side + px, side), :] = edge
    for b in range(3):
        dm[b, pl.ds(0, side), :] = edge
        dm[b, pl.ds(side + px, side), :] = edge
    for pay, real in ((pay1, real_k), (pay2, real_k), (payp, real_p)):
        rest = pay.shape[0] - real
        if rest:
            pay[pl.ds(real, rest), :] = jnp.zeros((rest, LANES), BF)
    wo[pl.ds(chans, WIN - own_chans), :] = jnp.zeros((WIN - own_chans, chans), BF)
    for h in range(heads):
        dot_t[h, pl.ds(HEAD_DIM, HEAD_DIM), :] = jnp.zeros((HEAD_DIM, px), BF)
    att_t[pl.ds(own_chans, WIN - own_chans), :] = jnp.zeros((WIN - own_chans, px), BF)
    vx[...] = jnp.zeros(vx.shape, F32)

    pl.semaphore_wait(barrier, len(peers))

    def swap(src, dst, k):
        cp = pltpu.make_async_remote_copy(
            src_ref=src, dst_ref=dst, send_sem=xs.at[k], recv_sem=xr.at[k], device_id=(img, oc), device_id_type=MESH
        )
        cp.start()
        return cp

    swap_x = swap(x_in.at[:, owin], xw.at[my_rows], 0)
    swap_g = swap(g_in, gf.at[my_rows], 1)

    lane1 = lax.broadcasted_iota(jnp.int32, (1, LANES), 1)
    low1 = lane1 < HEAD_DIM
    load_wi.wait()
    for k in range(3 * heads):
        place = 3 * heads * c + k
        blk = dqkv[pl.ds(0, chans), pl.ds(aligned((place // 2) * LANES, LANES), LANES)].astype(F32)
        blk = jnp.where(place % 2 == 0, blk, pltpu.roll(blk, HEAD_DIM, 1))
        wq[:, pl.ds(k * LANES, LANES)] = jnp.where(low1, blk, 0.0).astype(BF)

    for cp in small:
        cp.wait()

    def pvec(ref):
        return ref[win].reshape(1, WIN)

    gain1, shift1, offset1 = pvec(p_g1), pvec(p_s1), pvec(p_o1)
    gain2, shift2, offset2 = pvec(p_g2), pvec(p_s2), pvec(p_o2)
    gain3, shift3 = pvec(p_g3), pvec(p_s3)

    load_ew.wait()
    t = t_act[...]
    t_a = t.astype(BF).astype(F32)
    t_b = (t - t_a).astype(BF).astype(F32)
    row16 = lax.broadcasted_iota(jnp.int32, (16, t.shape[1]), 0)
    t_rows = jnp.where(row16 == 0, t_a, jnp.where(row16 == 1, t_b, jnp.where(row16 == 2, t - t_a - t_b, 0.0)))
    film[...] = total(dot(t_rows.astype(BF), ew[...])) + e_off[...].reshape(1, -1)
    scale2 = 1.0 + film[:, win]
    move2 = film[:, pl.ds(aligned(chans + LANES * c, LANES), WIN)]

    def stats_step(v, m, carry):
        vm = v * m
        return carry[0] + fold(vm), carry[1] + fold(vm * v)

    def moments(carry):
        s, q = group_totals(*carry)
        mean = s * inv_entries
        return mean, lax.rsqrt(q * inv_entries - mean * mean + EPSILON)

    def body(j, carry, at=0):
        j = j + at
        return stats_step(xw[rows_at(j, RC), :].astype(F32), mask2(j), carry)

    steps = half // RC
    load_x.wait()
    carry = lax.fori_loop(0, steps, functools.partial(body, at=steps * c), (zero8, zero8))
    swap_x.wait()
    mean1, rstd1 = moments(lax.fori_loop(0, steps, functools.partial(body, at=steps * oc), carry))
    mul1 = rstd1 * gain1
    add1 = shift1 - mean1 * mul1

    def body(j, _):
        pre = xw[rows_at(j, RC), :].astype(F32) * mul1 + add1
        act1[c, pad_at(j, RC), :] = (pre * sigmoid(pre) * own_f).astype(BF)
        return 0

    lax.fori_loop(0, px // RC, body, 0)
    inner = pl.ds(side, px)
    swap_a1 = swap(act1.at[c, inner], act1.at[c, inner], 2)

    col = lax.broadcasted_iota(jnp.int32, (MC, WIN), 0) % side
    not_first = (col != 0).astype(F32)
    not_last = (col != side - 1).astype(F32)

    def conv(acts, s, kern, back, j):
        accs = []
        for b in range(3):
            acc = None
            for a in range(3):
                lhs = acts[s, pl.ds(aligned(j * MC + side * a, 32), MC), :]
                if back:
                    tap = (2 - a) * 3 + 2 - b
                    rhs = kern[pl.ds(aligned(tap * chans + LANES * c, LANES), WIN), pl.ds(aligned(LANES * s, LANES), WIN)]
                    o = dot_nt(lhs, rhs)
                else:
                    tap = a * 3 + b
                    rhs = kern[pl.ds(aligned(tap * chans + LANES * s, LANES), WIN), win]
                    o = dot(lhs, rhs)
                acc = o if acc is None else acc + o
            accs.append(acc)
        return accs[1] + pltpu.roll(accs[0], 1, 0) * not_first + pltpu.roll(accs[2], MC - 1, 0) * not_last

    def turn(acts, shift, dst):
        def body(j, _):
            a0 = acts[0, pad_at(j, TC, shift), :].astype(F32)
            a1 = acts[1, pad_at(j, TC, shift), :].astype(F32)
            at = rows_at(j, TC)
            dst[pl.ds(0, LANES), at] = a0[:, :LANES].T.astype(BF)
            dst[pl.ds(LANES, LANES), at] = (a0[:, LANES:] + a1[:, :LANES]).T.astype(BF)
            dst[pl.ds(2 * LANES, LANES), at] = a1[:, LANES:].T.astype(BF)
            return 0

        lax.fori_loop(0, px // TC, body, 0)

    load_k1.wait()

    def body(j, _):
        cv[rows_at(j, MC), :] = conv(act1, c, k1, False, j)
        return 0

    lax.fori_loop(0, px // MC, body, 0, unroll=True)
    swap_a1.wait()

    def body(j, carry):
        v = cv[rows_at(j, MC), :] + conv(act1, oc, k1, False, j) + offset1
        cv[rows_at(j, MC), :] = v
        return stats_step(v, mask2(j, MC), carry)

    mean2, rstd2 = moments(lax.fori_loop(0, px // MC, body, (zero8, zero8), unroll=True))
    mul2 = rstd2 * gain2 * scale2
    add2 = (shift2 - mean2 * rstd2 * gain2) * scale2 + move2

    def body(j, _):
        pre = cv[rows_at(j, RC), :] * mul2 + add2
        act2[c, pad_at(j, RC), :] = (pre * sigmoid(pre) * own_f).astype(BF)
        return 0

    lax.fori_loop(0, px // RC, body, 0)
    swap_a2 = swap(act2.at[c, inner], act2.at[c, inner], 3)

    load_k2.wait()

    def body(j, _):
        at = rows_at(j, MC)
        hid[at, :] = conv(act2, c, k2, False, j) + offset2 + xw[at, :].astype(F32)
        return 0

    lax.fori_loop(0, px // MC, body, 0, unroll=True)
    swap_a2.wait()

    def body(j, carry):
        v = hid[rows_at(j, MC), :] + conv(act2, oc, k2, False, j)
        hid[rows_at(j, MC), :] = v
        return stats_step(v, mask2(j, MC), carry)

    mean3, rstd3 = moments(lax.fori_loop(0, px // MC, body, (zero8, zero8), unroll=True))
    mul3 = rstd3 * gain3
    add3 = shift3 - mean3 * mul3

    def body(j, _):
        act3[c, rows_at(j, RC), :] = ((hid[rows_at(j, RC), :] * mul3 + add3) * own_f).astype(BF)
        return 0

    lax.fori_loop(0, px // RC, body, 0)
    swap_a3 = swap(act3.at[c], act3.at[c], 4)

    biases = []
    for h in range(heads):
        blk = off_in[pl.ds(aligned(LANES * (heads * c + h), LANES), LANES)].reshape(1, LANES)
        turned = pltpu.roll(jnp.broadcast_to(blk, (8, LANES)), HEAD_DIM, 1)[:1]
        bias_q = jnp.where(low1, blk, jnp.where(lane1 == HEAD_DIM, 8.0, 0.0))
        bias_v = jnp.where(low1, turned, jnp.where(lane1 < HEAD_DIM + 2, 1.0, 0.0))
        biases.append((bias_q, bias_v))
    load_wo.wait()
    load_g.wait()
    swap_g.wait()
    wo_rows = pl.ds(aligned(own_chans * c, HEAD_DIM), own_chans)

    def body(j, _):
        o = dot_nt(wo[wo_rows, :], gf[rows_at(j, MC), :])
        for h in range(heads):
            dot_t[h, pl.ds(0, HEAD_DIM), rows_at(j, MC)] = o[HEAD_DIM * h : HEAD_DIM * (h + 1)].astype(BF)
        return 0

    lax.fori_loop(0, px // MC, body, 0, unroll=True)

    turn(act1, side, act_t1)
    turn(act2, side, act_t2)
    swap_a3.wait()

    def body(j, _):
        at = rows_at(j, MC)
        a0 = act3[0, at, :]
        a1 = act3[1, at, :]
        hidden_key = (mask[at, :] == 0.0) & (lane1 == HEAD_DIM)
        for h in range(heads):
            cols = pl.ds(3 * LANES * h, 3 * LANES)
            o = dot(a0, wq[pl.ds(0, WIN), cols]) + dot(a1, wq[pl.ds(LANES, WIN), cols])
            q = (o[:, :LANES] + biases[h][0]).astype(BF).astype(F32) * 0.125
            k = jnp.where(hidden_key, MASKED, o[:, LANES : 2 * LANES])
            v = o[:, 2 * LANES :] + biases[h][1]
            qa[h, at, :] = q.astype(BF)
            ka[h, at, :] = k.astype(BF)
            va[h, at, :] = v.astype(BF)
            kat[h, :, at] = k.T.astype(BF)
            vat[h, :, at] = v.T.astype(BF)
        return 0

    lax.fori_loop(0, px // MC, body, 0, unroll=True)

    row128 = lax.broadcasted_iota(jnp.int32, (LANES, px), 0)

    def body(h, _):
        qc = qa[h]
        scores = dot_nt(ka[h], qc)
        top = jnp.max(scores, axis=0, keepdims=True)
        e = jnp.exp(scores - top).astype(BF)
        o = dot(vat[h], e)
        inv = 1.0 / o[HEAD_DIM : HEAD_DIM + 1, :]
        o = o * inv
        att_t[pl.ds(aligned(HEAD_DIM * h, HEAD_DIM), HEAD_DIM), :] = o[:HEAD_DIM].astype(BF)
        g = dot_t[h].astype(F32)
        less = -inv * jnp.sum(g * o, axis=0, keepdims=True)
        high = less.astype(BF).astype(F32)
        g = jnp.where(row128 == HEAD_DIM, high, jnp.where(row128 == HEAD_DIM + 1, less - high, g * inv)).astype(BF)
        ds = (e.astype(F32) * dot(va[h], g)).astype(BF)
        grads = (dot(kat[h], ds).T * 0.125, dot(ds, qc), dot_nt(e, g))
        for k, d in enumerate(grads):
            dqkv[:, pl.ds(aligned((3 * h + k) * LANES, LANES), LANES)] = jnp.where(low1, d, 0.0).astype(BF)
        return 0

    lax.fori_loop(0, heads, body, 0, unroll=True)

    def body(j, _):
        at = rows_at(j, MC)
        datt_s[at, :] = dot_nt(dqkv[at, :], wq[owin, :]).astype(BF)
        return 0

    lax.fori_loop(0, px // MC, body, 0, unroll=True)
    swap_da = swap(datt_s, datt_r, 5)

    def body(j, _):
        at = rows_at(j, MC)
        tmp[at, :] = dot_nt(dqkv[at, :], wq[win, :])
        return 0

    lax.fori_loop(0, px // MC, body, 0, unroll=True)
    turn(act3, 0, act_t3)

    used = [0]
    flows = {}

    def flow_of(key, pay, rbuf, gathered, order, base, size):
        if size:
            flow = Flow(pay, rbuf, gathered, base, size, stages(order), (fs, fr, used[0]), c, img)
            used[0] += flow_sems
            flows[key] = flow
            flow.advance()

    def advance(point):
        for key in PLAN[point]:
            if key in flows:
                flows[key].advance()

    def hand_out(key):
        flow = flows.pop(key)
        for cp in flow.forwards:
            cp.wait()

    swap_da.wait()

    def back_sums(carry, u, normed):
        return carry[0] + fold(u), carry[1] + fold(u * normed)

    def body(j, carry):
        at = rows_at(j, RC)
        u = tmp[at, :] + datt_r[at, :].astype(F32)
        tmp[at, :] = u
        return back_sums(carry, u, (hid[at, :] - mean3) * rstd3)

    s0, s1 = lax.fori_loop(0, px // RC, body, (zero8, zero8))
    vx[pl.ds(6, 1), win] = total(s1) * own_f
    vx[pl.ds(7, 1), win] = total(s0) * own_f

    def spread_of(s0, s1, gain):
        a, b = group_totals(s0 * gain, s1 * gain)
        return a * inv_entries, b * inv_entries

    sp_a, sp_b = spread_of(s0, s1, gain3)

    def body(j, carry):
        at = rows_at(j, RC)
        normed = (hid[at, :] - mean3) * rstd3
        d = gf[at, win].astype(F32) + rstd3 * (tmp[at, :] * gain3 - mask2(j) * (sp_a + normed * sp_b))
        resid[at, :] = d
        low = (d * own_f).astype(BF)
        dd2[c, pad_at(j, RC), :] = low
        return carry + fold(low.astype(F32))

    vx[pl.ds(5, 1), win] = total(lax.fori_loop(0, px // RC, body, zero8))
    swap_d2 = swap(dd2.at[c, inner], dd2.at[c, inner], 7)

    own_lanes = pl.ds(aligned(LANES * c, LANES), LANES)
    mid_lanes = pl.ds(aligned(LANES * oc, LANES), LANES)
    hc = chans // 2
    my_half = pl.ds(aligned(hc * c, HEAD_DIM), hc)

    def shift_into(first_lane, read):
        lanes = pl.ds(first_lane, LANES)

        def body(j, _):
            at = pad_at(j, TC)
            d = read(at)
            dm[0, at, lanes] = (pltpu.roll(d, TC - 1, 0) * not_last[:TC, :LANES]).astype(BF)
            dm[1, at, lanes] = d.astype(BF)
            dm[2, at, lanes] = (pltpu.roll(d, 1, 0) * not_first[:TC, :LANES]).astype(BF)
            return 0

        lax.fori_loop(0, px // TC, body, 0)

    def kernel_grad(act_t, dd, wait, key, pay, rbuf, gathered, point):
        unit = 16 * n_img
        sizes = [units * unit for units in shares(pay.shape[0] // unit, KERNEL_FLOWS)]
        begun = []

        def begin(rows):
            while len(begun) < len(sizes) and sum(sizes[: len(begun) + 1]) <= rows:
                k = len(begun)
                flow_of(key + k, pay, rbuf, gathered, KERNEL_FLOWS[k][0], sum(sizes[:k]), sizes[k])
                begun.append(k)

        def tap_rows(tap, lanes):
            return dm[tap % 3, pl.ds(side * (2 - tap // 3), px), lanes]

        def block(rows, base, lanes):
            n = rows.shape[0]
            for tap in range(0, 9, 2):
                if tap < 8:
                    o = dot(rows[...], jnp.concatenate([tap_rows(tap, lanes), tap_rows(tap + 1, lanes)], axis=1))
                    pay[pl.ds(base + tap * n, n), :] = o[:, :LANES].astype(BF)
                    pay[pl.ds(base + (tap + 1) * n, n), :] = o[:, LANES:].astype(BF)
                else:
                    pay[pl.ds(base + tap * n, n), :] = dot(rows[...], tap_rows(tap, lanes)).astype(BF)
                begin(base + min(tap + 2, 9) * n)

        shift_into(0, lambda at: dd[c, at, own_lanes].astype(F32))
        block(act_t, 0, pl.ds(0, LANES))
        if point is not None:
            advance(point)
        wait()
        shift_into(LANES, lambda at: dd[c, at, mid_lanes].astype(F32) + dd[oc, at, own_lanes].astype(F32))
        block(act_t.at[my_half], 9 * chans, pl.ds(LANES, LANES))
        begin(pay.shape[0])

    kernel_grad(act_t2, dd2, swap_d2.wait, SECOND[0], pay2, rb2, out2, None)

    def body(j, carry):
        at = rows_at(j, MC)
        pre = cv[at, :] * mul2 + add2
        sg = sigmoid(pre)
        u = (conv(dd2, c, k2, True, j) + conv(dd2, oc, k2, True, j)) * (sg * (1.0 + pre * (1.0 - sg)))
        tmp[at, :] = u
        return back_sums(carry, u, (cv[at, :] - mean2) * rstd2)

    s0, s1 = lax.fori_loop(0, px // MC, body, (zero8, zero8), unroll=True)
    advance(0)
    t0, t1 = total(s0), total(s1)
    vx[pl.ds(9, 1), win] = (gain2 * t1 + shift2 * t0) * own_f
    vx[pl.ds(10, 1), win] = t0 * own_f
    vx[pl.ds(3, 1), win] = scale2 * t1 * own_f
    vx[pl.ds(4, 1), win] = scale2 * t0 * own_f
    gain2s = gain2 * scale2
    sp_a, sp_b = spread_of(s0, s1, gain2s)

    def body(j, carry):
        at = rows_at(j, RC)
        normed = (cv[at, :] - mean2) * rstd2
        d = rstd2 * (tmp[at, :] * gain2s - mask2(j) * (sp_a + normed * sp_b))
        low = (d * own_f).astype(BF)
        dd1[c, pad_at(j, RC), :] = low
        return carry + fold(low.astype(F32))

    vx[pl.ds(2, 1), win] = total(lax.fori_loop(0, px // RC, body, zero8))
    swap_d1 = swap(dd1.at[c, inner], dd1.at[c, inner], 8)

    advance(1)

    kernel_grad(act_t1, dd1, swap_d1.wait, FIRST[0], pay1, rb1, out1, 2)
    advance(3)

    for k in range(3 * heads // 2):
        o = dot(act_t3[...], dqkv[:, pl.ds(2 * LANES * k, 2 * LANES)])
        pair = o[:, :LANES] + pltpu.roll(o[:, LANES:], HEAD_DIM, 1)
        payp[pl.ds(k * chans, chans), :] = pair.astype(BF)
    base = (3 * heads // 2) * chans
    if (3 * heads) % 2:
        o = dot(act_t3[...], dqkv[:, pl.ds((3 * heads - 1) * LANES, LANES)])
        pair = o[: chans // 2] + pltpu.roll(o[chans // 2 :], HEAD_DIM, 1)
        payp[pl.ds(base, chans // 2), :] = pair.astype(BF)
        base += chans // 2
    o = dot(att_t[pl.ds(0, own_chans), :], gf[...])
    for b in range(chans // LANES):
        payp[pl.ds(base + b * own_chans, own_chans), :] = o[:, b * LANES : (b + 1) * LANES].astype(BF)

    for h in range(heads):
        z = jnp.zeros((8, LANES), F32)

        def body(j, carry, h=h):
            at = rows_at(j, TC)
            q = dqkv[at, pl.ds(3 * h * LANES, LANES)].astype(F32)
            v = dqkv[at, pl.ds((3 * h + 2) * LANES, LANES)].astype(F32)
            return carry[0] + fold(q), carry[1] + fold(v)

        sum_q, sum_v = lax.fori_loop(0, px // TC, body, (z, z))
        sums = total(sum_q + pltpu.roll(sum_v, HEAD_DIM, 1))
        vx[pl.ds(13, 1), pl.ds(LANES * h, LANES)] = jnp.where(first, sums, 0.0)
        vx[pl.ds(14, 1), pl.ds(LANES * h, LANES)] = jnp.where(first, 0.0, sums)

    advance(4)
    at = 0
    for k, units in enumerate(shares(payp.shape[0] // (16 * n_img), PROJECT_FLOWS)):
        flow_of(PROJECT[0] + k, payp, rbp, outp, PROJECT_FLOWS[k][0], at, units * 16 * n_img)
        at += units * 16 * n_img

    def body(j, carry):
        at = rows_at(j, MC)
        x = xw[at, :].astype(F32)
        pre = x * mul1 + add1
        sg = sigmoid(pre)
        u = (conv(dd1, c, k1, True, j) + conv(dd1, oc, k1, True, j)) * (sg * (1.0 + pre * (1.0 - sg)))
        tmp[at, :] = u
        return back_sums(carry, u, (x - mean1) * rstd1)

    s0, s1 = lax.fori_loop(0, px // MC, body, (zero8, zero8), unroll=True)
    advance(5)
    vx[pl.ds(0, 1), win] = total(s1) * own_f
    vx[pl.ds(1, 1), win] = total(s0) * own_f

    g_sum = jnp.zeros((8, chans), F32)

    def body(j, carry):
        return carry + fold(gf[rows_at(j, RC), :].astype(F32))

    g_sum = total(lax.fori_loop(0, px // RC, body, g_sum))
    vx[pl.ds(8, 1), :] = jnp.where(first, g_sum, 0.0)
    for k in range(2):
        vx[pl.ds(11 + k, 1), :] = jnp.where(first, t_act[:, pl.ds(k * chans, chans)], 0.0)
    swap_v = swap(vx, vr, 9)

    sp_a, sp_b = spread_of(s0, s1, gain1)

    def body(j, _):
        at = rows_at(j, RC)
        normed = (xw[at, :].astype(F32) - mean1) * rstd1
        d = resid[at, :] + rstd1 * (tmp[at, :] * gain1 - mask2(j) * (sp_a + normed * sp_b))
        tmp[at, :] = d * own_f
        datt_s[at, :] = (d * own_f).astype(BF)
        return 0

    lax.fori_loop(0, px // RC, body, 0)
    swap_i = swap(datt_s.at[other_rows], ing_r, 10)

    swap_v.wait()
    vall[img] = vx[...] + vr[...]

    class Gather:
        def __init__(self):
            self.k = -1
            self.copies = []

        def advance(self):
            for cp in self.copies:
                cp.wait()
            self.copies = []
            self.k += 1
            if self.k < nbits:
                bit = bits[self.k]
                at = vall.at[pl.ds((img // bit) * bit, bit)]
                k = used[0]
                used[0] += 1
                cp = pltpu.make_async_remote_copy(
                    src_ref=at, dst_ref=at, send_sem=fs.at[k], recv_sem=fr.at[k],
                    device_id=(xor(img, [bit], 1), c), device_id_type=MESH,
                )
                cp.start()
                self.copies.append(cp)

    vectors = Gather()
    vectors.advance()
    advance(6)

    def body(j, _):
        at = rows_at(j, TC)
        tsum[at, :] = dot(att_t[:, at].astype(F32).T.astype(BF), wo[pl.ds(aligned(own_chans * c, HEAD_DIM), WIN), :])
        tsum[at, win] += hid[at, :] * own_f
        return 0

    lax.fori_loop(0, px // TC, body, 0)
    swap_t = swap(tsum.at[other_rows], trecv, 6)

    advance(7)
    vectors.advance()

    swap_t.wait()
    res_v[...] = (tsum[my_rows, :] + trecv[...] + p_oo[...].reshape(1, -1)).astype(BF)
    swap_i.wait()
    top_rows = pl.ds(0, half)
    tsum[top_rows, :] = jnp.zeros((half, chans), F32)
    tsum[top_rows, win] = tmp[my_rows, :]
    tsum[top_rows, owin] += ing_r[...].astype(F32)
    ing_v[...] = tsum[top_rows, :].astype(BF)
    ended = {}
    for n, key in enumerate(PLAN[8]):
        if key in flows:
            flows[key].advance()
            if flows[key].ended():
                ended.setdefault(key, n)
        if n % 8 == 7:
            vectors.advance()
        for key in [k for k in ended if ended[k] + 6 == n]:
            hand_out(key)
    while any(not flow.ended() for flow in flows.values()):
        for flow in flows.values():
            flow.advance()
        vectors.advance()
    while vectors.copies:
        vectors.advance()
    for key in sorted(flows, key=lambda k: ended.get(k, 0)):
        hand_out(key)


def finish_kernel(dims, b1, b2, bp, bv, res, ing, *refs):
    chans, heads = dims
    (res_o, ing_o, g1, s1, k1o, o1, ewo, eoo, g2, s2, k2o, o2, g3, s3, pio, oio, poo, ooo) = refs[:18]
    (f1, f2, fe, fi, fo, fw, fv, osem) = refs[18:]
    hc = chans // 2
    own = chans // 2
    te = fe.shape[0]

    def move(src, dst, sem):
        cp = pltpu.make_async_copy(src, dst, sem)
        cp.start()
        return cp

    out = [move(res, res_o, osem.at[0]), move(ing, ing_o, osem.at[1])]

    def kernel(n, pay, full, dst):
        for a in range(3):

            def body(b, _, a=a):
                tap = 3 * a + b
                at = main = pl.ds(pl.multiple_of(tap * chans, LANES), chans)
                full[at, pl.ds(0, LANES)] = pay[0, main, :].astype(F32)
                full[at, pl.ds(2 * LANES, LANES)] = pay[1, main, :].astype(F32)
                mid = pl.ds(pl.multiple_of(9 * chans + tap * hc, HEAD_DIM), hc)
                for s in range(2):
                    to = pl.ds(pl.multiple_of(tap * chans + s * hc, HEAD_DIM), hc)
                    full[to, pl.ds(LANES, LANES)] = pay[s, mid, :].astype(F32)
                return 0

            lax.fori_loop(0, 3, body, 0)
            part = pl.ds(3 * a * chans, 3 * chans)
            out.append(move(full.at[part], dst.at[part], osem.at[3 + 3 * n + a]))

    kernel(0, b2, f2, k2o)

    sums = jnp.sum(bv[...], axis=0)
    for n, (dst, k) in enumerate(((g1, 0), (s1, 1), (o1, 2), (g2, 3), (s2, 4), (o2, 5), (g3, 6), (s3, 7), (ooo, 8))):
        at = pl.ds(n * chans, chans)
        fv[at] = sums[k]
        out.append(move(fv.at[at], dst, osem.at[11 + n]))
    for n, (dst, k) in enumerate(((eoo, 9), (oio, 13))):
        at = pl.ds(2 * n * chans, 2 * chans)
        fw[pl.ds(2 * n * chans, chans)] = sums[k]
        fw[pl.ds((2 * n + 1) * chans, chans)] = sums[k + 1]
        out.append(move(fw.at[at], dst, osem.at[20 + n]))
    for a in range(2):
        for b in range(2):
            fe[pl.ds(a * chans, chans), pl.ds(b * chans, chans)] = lax.dot_general(
                bv[:, 11 + a, :], bv[:, 9 + b, :], (((0,), (0,)), ((), ())),
                preferred_element_type=F32, precision=lax.Precision.HIGHEST,
            )
    out.append(move(fe, ewo, osem.at[2]))

    kernel(1, b1, f1, k1o)

    low = lax.broadcasted_iota(jnp.int32, (1, LANES), 1) < HEAD_DIM
    pairs = 3 * heads // 2
    odd = (3 * heads) % 2
    sides = []
    for s in range(2):
        blocks = [bp[s, pl.ds(k * chans, chans), :].astype(F32) for k in range(pairs)]
        if odd:
            last = bp[s, pl.ds(pairs * chans, chans // 2), :].astype(F32)
            blocks.append(jnp.concatenate([last, pltpu.roll(last, HEAD_DIM, 1)], axis=0))
        sides.append(blocks)
    cols = sides[0] + sides[1]
    if odd:
        turned = [pltpu.roll(b, HEAD_DIM, 1) for b in sides[1]]
        cols = sides[0][:-1] + [jnp.where(low, sides[0][-1], turned[0])]
        cols += [jnp.where(low, turned[k], turned[k + 1]) for k in range(pairs)]
    for k, b in enumerate(cols):
        fi[:, pl.ds(k * LANES, LANES)] = b
    out.append(move(fi, pio, osem.at[9]))
    base = pairs * chans + odd * (chans // 2)
    for s in range(2):
        for b in range(chans // LANES):
            fo[pl.ds(s * own, own), pl.ds(b * LANES, LANES)] = bp[s, pl.ds(base + b * own, own), :].astype(F32)
    out.append(move(fo, poo, osem.at[10]))
    for cp in out:
        cp.wait()


def time_features(timesteps, width):
    half_width = width // 2
    frequency = jnp.exp(-math.log(10000.0) * jnp.arange(half_width, dtype=jnp.float32) / half_width)
    angles = timesteps.astype(jnp.float32)[:, None] * frequency[None, :]
    return jnp.concatenate([jnp.cos(angles), jnp.sin(angles)], axis=1)


def local(
    n_img,
    images_in, extents, timesteps, gain_first, shift_first, kernel_first, offset_first, embed_weight, embed_offset,
    gain_second, shift_second, kernel_second, offset_second, gain_attend, shift_attend, project_in, offset_in,
    project_out, offset_out, out_grad,
):
    _, stripe_rows, side, chans = images_in.shape
    px = side * side
    half = stripe_rows * side
    te = embed_weight.shape[0]
    own = chans // 2
    heads = own // HEAD_DIM
    taps = 9
    unit = 16 * n_img
    real_k = taps * (chans + chans // 2)
    real_p = 3 * heads * HEAD_DIM * chans // LANES + own * (chans // LANES)
    rows_k = cdiv(real_k, unit) * unit
    rows_p = cdiv(real_p, unit) * unit
    bits = []
    while 2 ** len(bits) < n_img:
        bits.append(2 ** len(bits))
    nbits = len(bits)

    t_act = jax.nn.silu(time_features(timesteps, te))
    vm = pl.BlockSpec(memory_space=pltpu.VMEM)
    anym = pl.BlockSpec(memory_space=pl.ANY)
    smem = pl.BlockSpec(memory_space=pltpu.SMEM)
    sds = jax.ShapeDtypeStruct
    V = pltpu.VMEM
    padded = px + 2 * side
    wide = 3 * heads * LANES
    flow_sems = 2 * nbits + 2
    n_sem = (2 * len(KERNEL_FLOWS) + len(PROJECT_FLOWS)) * flow_sems + nbits
    scratch = [
        V((taps * chans, chans), BF), V((taps * chans, chans), BF),
        V((chans + WIN - own, chans), BF), V((te, 2 * chans), BF), V((chans, wide), BF),
        V((px, WIN), BF), V((px, chans), BF), V((px, LANES), F32), V((1, 2 * chans), F32),
        V((2, padded, WIN), BF), V((2, padded, WIN), BF), V((2, px, WIN), BF), V((2, padded, WIN), BF), V((2, padded, WIN), BF),
        V((px, WIN), F32), V((px, WIN), F32), V((px, WIN), F32), V((px, WIN), F32),
        V((heads, px, LANES), BF), V((heads, px, LANES), BF), V((heads, px, LANES), BF),
        V((heads, LANES, px), BF), V((heads, LANES, px), BF), V((heads, LANES, px), BF), V((WIN, px), BF), V((px, wide), BF),
        V((px, chans), F32), V((half, chans), F32), V((px, WIN), BF), V((px, WIN), BF),
        V((3, padded, WIN), BF), V((chans, px), BF), V((chans, px), BF), V((chans, px), BF), V((half, WIN), BF),
        V((rows_k, LANES), BF), V((rows_k, LANES), BF), V((rows_p, LANES), BF),
        V((rows_k, LANES), BF), V((rows_k, LANES), BF), V((rows_p, LANES), BF),
        V((16, chans), F32), V((16, chans), F32),
        V((chans,), F32), V((chans,), F32), V((chans,), F32), V((chans,), F32), V((chans,), F32), V((chans,), F32), V((chans,), F32), V((chans,), F32), V((chans,), F32), V((1, 2 * chans), F32), V((2 * chans,), F32), V((2 * chans,), F32),
        pltpu.SemaphoreType.DMA((19,)), pltpu.SemaphoreType.DMA((11,)), pltpu.SemaphoreType.DMA((11,)),
        pltpu.SemaphoreType.DMA((n_sem,)), pltpu.SemaphoreType.DMA((n_sem,)),
    ]
    res, ing, pk1, pk2, pp, vec = pl.pallas_call(
        functools.partial(block_kernel, (side, chans, n_img, real_k, real_p, tuple(bits), flow_sems)),
        out_shape=(
            V((half, chans), BF), V((half, chans), BF), V((2, rows_k, LANES), BF), V((2, rows_k, LANES), BF),
            V((2, rows_p, LANES), BF), V((n_img, 16, chans), F32),
        ),
        in_specs=[anym, anym, smem] + [anym] * 12 + [anym, anym, anym, anym, anym],
        out_specs=(vm,) * 6,
        scratch_shapes=scratch,
        compiler_params=pltpu.CompilerParams(collective_id=0, has_side_effects=True, vmem_limit_bytes=50 * 2**20),
        cost_estimate=pl.CostEstimate(flops=2 * 10**10, bytes_accessed=2 * 10**7, transcendentals=4 * 10**6),
        name="block",
    )(
        images_in.reshape(half, chans), out_grad.reshape(half, chans), extents, gain_first, shift_first, offset_first,
        gain_second, shift_second, offset_second, gain_attend, shift_attend, offset_out, t_act, embed_offset, offset_in,
        kernel_first.reshape(taps * chans, chans), kernel_second.reshape(taps * chans, chans),
        project_in, project_out, embed_weight,
    )

    row = sds((chans,), F32)
    row2 = sds((2 * chans,), F32)
    kern = sds((taps * chans, chans), F32)
    stripe = sds((half, chans), BF)
    outs = pl.pallas_call(
        functools.partial(finish_kernel, (chans, heads)),
        out_shape=(
            stripe, stripe, row, row, kern, row, sds((te, 2 * chans), F32), row2, row, row, kern, row, row, row,
            sds((chans, 3 * chans), F32), row2, sds((chans, chans), F32), row,
        ),
        in_specs=[vm] * 6,
        out_specs=(anym,) * 18,
        scratch_shapes=[
            V((taps * chans, chans), F32), V((taps * chans, chans), F32), V((te, 2 * chans), F32),
            V((chans, 3 * chans), F32), V((chans, chans), F32), V((4 * chans,), F32), V((9 * chans,), F32),
            pltpu.SemaphoreType.DMA((22,)),
        ],
        compiler_params=pltpu.CompilerParams(vmem_limit_bytes=32 * 2**20),
        cost_estimate=pl.CostEstimate(flops=10**8, bytes_accessed=23 * 10**6, transcendentals=0),
        name="finish",
    )(*(pltpu.with_memory_space_constraint(x, pltpu.VMEM) for x in (pk1, pk2, pp, vec, res, ing)))
    res, ing, *outs = outs
    shapes = (
        gain_first, shift_first, kernel_first, offset_first, embed_weight, embed_offset, gain_second, shift_second,
        kernel_second, offset_second, gain_attend, shift_attend, project_in, offset_in, project_out, offset_out,
    )
    outs = [o.reshape(s.shape) for o, s in zip(outs, shapes)]
    return (res.reshape(images_in.shape), ing.reshape(images_in.shape), *outs)


def solution(mesh):
    n_img = mesh.shape["img"]
    stripe = P("img", "pix", None, None)
    in_specs = (stripe, P("img", None), P("img")) + (P(),) * 16 + (stripe,)
    out_specs = (stripe, stripe) + (P(),) * 16
    return jax.shard_map(
        functools.partial(local, n_img), mesh=mesh, in_specs=in_specs, out_specs=out_specs, check_vma=False
    )
```
